32 devices in a mesh: dp: 8 (over y, x, core), mp: 4 (over z).
Axes of the slice: x: 2, y: 2, z: 4, core: 2. Of those that a mesh axis runs over, the one named last changes fastest.
Arguments:
- inputs: bfloat16 [16, 1024, 768], P('dp', 'mp'), may hold values from -6 to 6
- lengths: int32 [16], P('dp'), may hold values from 100 to 1024, as said below
- ln1_gain: float32 [768], replicated, may hold values from 0.25 to 1.75
- ln1_bias: float32 [768], replicated, may hold values from -4 to 4
- w_qkv: bfloat16 [3, 768, 768], P(None, None, 'mp'), may hold values from -0.21875 to 0.21875
- b_qkv: float32 [3, 768], P(None, 'mp'), may hold values from -4 to 4
- w_out: bfloat16 [768, 768], P('mp'), may hold values from -1.75 to 1.75
- b_out: float32 [768], replicated, may hold values from -4 to 4
- ln2_gain: float32 [768], replicated, may hold values from 0.25 to 1.75
- ln2_bias: float32 [768], replicated, may hold values from -4 to 4
- w_up: bfloat16 [768, 3072], P(None, 'mp'), may hold values from -0.21875 to 0.21875
- b_up: bfloat16 [3072], P('mp'), may hold values from -4 to 4
- w_down: bfloat16 [3072, 768], P('mp'), may hold values from -0.109375 to 0.109375
- b_down: float32 [768], replicated, may hold values from -4 to 4
- cotangent: bfloat16 [16, 1024, 768], P('dp', 'mp'), may hold values from -12 to 12
Outputs:
- layer_out: bfloat16 [16, 1024, 768], P('dp', 'mp')
- grad_inputs: float32 [16, 1024, 768], P('dp', 'mp')
- grad_ln1_gain: float32 [768], replicated
- grad_ln1_bias: float32 [768], replicated
- grad_w_qkv: float32 [3, 768, 768], P(None, None, 'mp')
- grad_b_qkv: float32 [3, 768], P(None, 'mp')
- grad_w_out: float32 [768, 768], P('mp')
- grad_b_out: float32 [768], replicated
- grad_ln2_gain: float32 [768], replicated
- grad_ln2_bias: float32 [768], replicated
- grad_w_up: float32 [768, 3072], P(None, 'mp')
- grad_b_up: float32 [3072], P('mp')
- grad_w_down: float32 [3072, 768], P('mp')
- grad_b_down: float32 [768], replicated
The draws below stay inside these ranges and needn't reach their ends.
Inputs may be any that keep to these rules, and one draw needn't show every extreme that they name: `lengths`: in each aligned block of 2 rows (the rows of one index of dp) one row, drawn from the seed, has all 1024 codons.
All inputs are finite; a program needn't handle non-finite values.
Results may differ from the reference program's by a relative error of at most 0.02.
Values may be sent and summed in bfloat16 or wider, within the bound.
A program may use at most 128 MiB of HBM per device.

```python
import math
import jax
import jax.numpy as jnp
from jax import lax

D = 768
HEADS = 12
HDIM = 64
FF = 3072
SEQ = 1024
MINLEN = 100
ROWS_DEV = 2
ROWS = 16


def draw_lengths(key, part):
    key = jax.random.fold_in(key, 11)
    key_one, key_two, key_three, key_pick = jax.random.split(key, 4)
    first = jax.random.randint(key_one, (ROWS,), MINLEN, SEQ + 1)
    second = jax.random.randint(key_two, (ROWS,), MINLEN, SEQ + 1)
    third = jax.random.randint(key_three, (ROWS,), MINLEN, SEQ + 1)
    shorter = jnp.minimum(jnp.minimum(first, second), third)
    chosen = jax.random.randint(key_pick, (ROWS // ROWS_DEV,), 0, ROWS_DEV)
    full_rows = (jnp.arange(ROWS_DEV, dtype=jnp.int32)[None, :] == chosen[:, None]).reshape(ROWS)
    return jnp.where(full_rows, SEQ, shorter).astype(jnp.int32)


def draw_cotangent(key, part):
    key = jax.random.fold_in(key, 23)
    rising = 1.0 + 2.0 * jnp.arange(ROWS, dtype=jnp.float32) / max(ROWS - 1, 1)
    base = jnp.clip(jax.random.normal(key, (ROWS, SEQ, D), jnp.float32), -4.0, 4.0)
    return (base * rising[:, None, None]).astype(jnp.bfloat16)


def block_scale(rng, shape, pieces, low, high):
    level = 1.0
    for axis_at, blocks in pieces:
        steps = jax.random.uniform(jax.random.fold_in(jax.random.fold_in(rng, 6), axis_at), (blocks,), jnp.float32, low / len(pieces), high / len(pieces))
        level = level * jnp.repeat(jnp.exp(steps), shape[axis_at] // blocks).reshape((-1,) + (1,) * (len(shape) - 1 - axis_at))
    return level


def normal_values(key, shape, scale, reach, shards=(), kind=jnp.bfloat16):
    result = scale * jax.random.normal(key, shape, jnp.float32)
    if shards:
        result = result * block_scale(key, shape, shards, -0.22, 0.18)
    return jnp.clip(result, -reach, reach).astype(kind)


def setup_inputs(seed: int = 0) -> dict:
    key_of = jax.random.split(jax.random.key(seed), 16)
    return {
        "inputs": normal_values(key_of[0], (ROWS, SEQ, D), 1.0, 6.0, ((0, 8), (1, 4))),
        "lengths": draw_lengths(jax.random.fold_in(key_of[15], 71), 0),
        "ln1_gain": jnp.clip(1.0 + 0.15 * jax.random.normal(key_of[2], (D,), jnp.float32), 0.25, 1.75),
        "ln1_bias": normal_values(key_of[3], (D,), 0.3, 4.0, (), jnp.float32),
        "w_qkv": normal_values(key_of[4], (3, D, D), D ** -0.5, 0.21875, ((2, 4),)),
        "b_qkv": normal_values(key_of[5], (3, D), 0.3, 4.0, ((1, 4),), jnp.float32),
        "w_out": normal_values(key_of[6], (D, D), (D // 64) ** -0.5, 1.75, ((0, 4),)),
        "b_out": normal_values(key_of[7], (D,), 0.3, 4.0, (), jnp.float32),
        "ln2_gain": jnp.clip(1.0 + 0.15 * jax.random.normal(key_of[8], (D,), jnp.float32), 0.25, 1.75),
        "ln2_bias": normal_values(key_of[9], (D,), 0.3, 4.0, (), jnp.float32),
        "w_up": normal_values(key_of[10], (D, FF), D ** -0.5, 0.21875, ((1, 4),)),
        "b_up": normal_values(key_of[11], (FF,), 0.3, 4.0, ((0, 4),)),
        "w_down": normal_values(key_of[12], (FF, D), FF ** -0.5, 0.109375, ((0, 4),)),
        "b_down": normal_values(key_of[13], (D,), 0.3, 4.0, (), jnp.float32),
        "cotangent": draw_cotangent(jax.random.fold_in(key_of[15], 71), 0),
    }


norm_eps = 1e-05
masked_score = -1000000000.0
highest = lax.Precision.HIGHEST

@jax.custom_vjp
def low(v):
    return lax.optimization_barrier(v.astype(jnp.bfloat16)).astype(jnp.float32)

@jax.custom_vjp
def low_back(v):
    return v

def low_keep(v):
    return (low(v), None)

def low_pass(kept, grad):
    return (grad,)

def back_keep(v):
    return (v, None)

def back_low(kept, grad):
    return (low(grad),)
low.defvjp(low_keep, low_pass)
low_back.defvjp(back_keep, back_low)

def layer_norm(values, gain_vec, bias_vec):
    middle = lax.optimization_barrier(jnp.mean(values, axis=-1, keepdims=True))
    centred = values - middle
    spread = lax.optimization_barrier(jnp.mean(centred * centred, axis=-1, keepdims=True))
    return centred * lax.rsqrt(spread + norm_eps) * gain_vec + bias_vec

def rotary_tables(seq_len, head_size):
    freq_steps = jnp.arange(head_size // 2, dtype=jnp.float32)
    frequency = jnp.exp(freq_steps * (-2.0 * math.log(10000.0) / head_size))
    angles = jnp.arange(seq_len, dtype=jnp.float32)[:, None] * frequency[None, :]
    cosine = jnp.concatenate([jnp.cos(angles), jnp.cos(angles)], -1)
    sine_table = jnp.concatenate([jnp.sin(angles), jnp.sin(angles)], -1)
    return (cosine, sine_table)

def rotate(values, cosine, sine_table):
    half_size = values.shape[-1] // 2
    turned = jnp.concatenate([-values[..., half_size:], values[..., :half_size]], -1)
    return values * cosine[:, None, :] + turned * sine_table[:, None, :]

def row_forward(input_row, length, g_one, c_one, w_proj, b_proj, w_mix, b_mix, g_two, c_two, w_hidden, b_hidden, w_back, b_back):
    keep_mask = jnp.arange(SEQ, dtype=jnp.int32) < length
    cosine, sine_table = rotary_tables(SEQ, HDIM)
    normed_one = low(layer_norm(input_row, g_one, c_one))
    qkv_raw = low_back(jnp.einsum('ld,tde->tle', normed_one, w_proj, precision=highest) + b_proj[:, None, :])
    queries = low(rotate(qkv_raw[0].reshape(SEQ, HEADS, HDIM), cosine, sine_table))
    key_rows = low(rotate(qkv_raw[1].reshape(SEQ, HEADS, HDIM), cosine, sine_table))
    value_rows = low(qkv_raw[2].reshape(SEQ, HEADS, HDIM))
    scores = low_back(jnp.einsum('qhe,khe->hqk', queries, key_rows, precision=highest) * HDIM ** (-0.5))
    scores = jnp.where(keep_mask[None, None, :], scores, masked_score)
    row_max = lax.optimization_barrier(jnp.max(scores, -1, keepdims=True))
    weights = jnp.exp(scores - row_max)
    probs = low(weights / lax.optimization_barrier(jnp.sum(weights, -1, keepdims=True)))
    mixed = jnp.einsum('hqk,khe->qhe', probs, value_rows, precision=highest).reshape(SEQ, D)
    mixed = low(low_back(mixed))
    attn_out = low_back(jnp.dot(mixed, w_mix, precision=highest) + b_mix)
    residual = input_row + attn_out
    normed_two = low(layer_norm(residual, g_two, c_two))
    up_value = low_back(jnp.dot(normed_two, w_hidden, precision=highest) + b_hidden)
    activation = low(jax.nn.gelu(up_value, approximate=False))
    down_out = low_back(jnp.dot(activation, w_back, precision=highest) + b_back)
    return (residual + down_out) * keep_mask[:, None].astype(residual.dtype)

def reference(inputs, lengths, ln1_gain, ln1_bias, w_qkv, b_qkv, w_out, b_out, ln2_gain, ln2_bias, w_up, b_up, w_down, b_down, cotangent):
    params = tuple((item.astype(jnp.float32) for item in (ln1_gain, ln1_bias, w_qkv, b_qkv, w_out, b_out, ln2_gain, ln2_bias, w_up, b_up, w_down, b_down)))

    def step(totals, scan_item):
        input_row, length, cotan_row = scan_item

        def run_row(row_value, *weight_list):
            return row_forward(row_value, length, *weight_list)
        out_row, pull_back = jax.vjp(run_row, input_row.astype(jnp.float32), *params)
        gradients = pull_back(cotan_row.astype(jnp.float32))
        totals = tuple((earlier + later for earlier, later in zip(totals, gradients[1:])))
        return (totals, (out_row.astype(jnp.bfloat16), gradients[0]))
    initial = tuple((jnp.zeros_like(item) for item in params))
    totals, outputs = lax.scan(step, initial, (inputs, lengths, cotangent))
    layer_out, grad_inputs = outputs
    return (layer_out, grad_inputs, totals[0], totals[1], totals[2], totals[3], totals[4], totals[5], totals[6], totals[7], totals[8], totals[9], totals[10], totals[11])
```

```python
import math

import jax
import jax.numpy as jnp
from jax import lax
from jax.sharding import PartitionSpec as P

HDIM = 64
norm_eps = 1e-05
masked_score = -1000000000.0
F32 = jnp.float32
BF16 = jnp.bfloat16


def rotary_tables(positions, head_size):
    freq_steps = jnp.arange(head_size // 2, dtype=F32)
    frequency = jnp.exp(freq_steps * (-2.0 * math.log(10000.0) / head_size))
    angles = positions.astype(F32)[:, None] * frequency[None, :]
    cosine = jnp.concatenate([jnp.cos(angles), jnp.cos(angles)], -1)
    sine_table = jnp.concatenate([jnp.sin(angles), jnp.sin(angles)], -1)
    return (cosine, sine_table)


def rotate(values, cosine, sine_table):
    half_size = values.shape[-1] // 2
    turned = jnp.concatenate([-values[..., half_size:], values[..., :half_size]], -1)
    return values * cosine[:, None, :] + turned * sine_table[:, None, :]


def rotate_back(grads_in, cosine, sine_table):
    half_size = grads_in.shape[-1] // 2
    scaled = grads_in * sine_table[:, None, :]
    turned = jnp.concatenate([scaled[..., half_size:], -scaled[..., :half_size]], -1)
    return grads_in * cosine[:, None, :] + turned


def gelu_slope(values):
    return (
        0.5 * (1.0 + lax.erf(values * 0.7071067811865476))
        + values * jnp.exp(-0.5 * values * values) * 0.3989422804014327
    )


def norm_stats(values):
    middle = jnp.mean(values, axis=-1, keepdims=True)
    centred = values - middle
    spread = jnp.mean(centred * centred, axis=-1, keepdims=True)
    scale = lax.rsqrt(spread + norm_eps)
    return centred * scale, scale


def norm_back(grad, unit, scale, gain):
    h = grad * gain
    return scale * (
        h
        - jnp.mean(h, axis=-1, keepdims=True)
        - unit * jnp.mean(h * unit, axis=-1, keepdims=True)
    )


class Links:
    def __init__(self):
        self.ndp = lax.axis_size("dp")
        self.nmp = lax.axis_size("mp")
        self.dp = lax.axis_index("dp")
        self.mp = lax.axis_index("mp")
        self.bits = self.ndp.bit_length() - 1
        self.low = min(3, self.bits)
        self.pieces = 1 << self.low

    def bit(self, b):
        return (self.dp >> b) & 1

    def pair(self, x, b):
        return lax.ppermute(x, "dp", [(i, i ^ (1 << b)) for i in range(self.ndp)])

    def across(self, x, j):
        return lax.ppermute(x, "mp", [(i, i ^ j) for i in range(self.nmp)])

    def row_perm(self, k, back):
        pairs = []
        for dp in range(self.ndp):
            for z in range(self.nmp):
                q, c = dp // 2, dp % 2
                src = dp * self.nmp + z
                dst = (2 * q + z // 2) * self.nmp + 2 * c + ((z % 2) ^ k)
                pairs.append((dst, src) if back else (src, dst))
        return pairs

    def to_rows(self, x):
        out = []
        for k in range(2):
            mine = lax.dynamic_index_in_dim(x, (self.mp % 2) ^ k, 0, keepdims=False)
            out.append(lax.ppermute(mine, ("dp", "mp"), self.row_perm(k, False)))
        return out

    def from_rows(self, blocks):
        got = [
            lax.ppermute(blocks[k], ("dp", "mp"), self.row_perm(k, True)) for k in range(2)
        ]
        odd = self.mp % 2 == 1
        return jnp.stack([jnp.where(odd, got[1], got[0]), jnp.where(odd, got[0], got[1])])

    def join(self, own, other, b, axis):
        return jnp.where(
            self.bit(b) == 1,
            jnp.concatenate([other, own], axis),
            jnp.concatenate([own, other], axis),
        )

    def orders(self):
        upper = list(range(1, self.low))
        return [upper, upper[::-1]]

    def gather_dp(self, piece):
        k, r, w = piece.shape
        halves = []
        for order, half in zip(self.orders(), (piece[:, : r // 2], piece[:, r // 2 :])):
            now = half.reshape((k,) + (1,) * self.low + (r // 2, w))
            for b in order + [0]:
                now = self.join(now, self.pair(now, b), b, 1 + self.low - 1 - b)
            halves.append(now)
        whole = jnp.concatenate(halves, axis=1 + self.low)
        return whole.reshape(k, self.pieces * r, w)

    def gather_weight(self, own):
        n, w = own.shape
        r = n // self.pieces
        mine = lax.dynamic_slice_in_dim(own, (self.dp % self.pieces) * r, r, 0)
        got = jnp.stack([self.across(mine, j) for j in range(1, self.nmp)])
        got = self.gather_dp(got)
        return self.by_mp([own] + [got[j] for j in range(self.nmp - 1)])

    def by_mp(self, items):
        stacked = jnp.stack(items)
        for b in range(self.nmp.bit_length() - 1):
            odd = ((self.mp >> b) & 1) == 1
            shape = stacked.shape
            high = self.nmp >> (b + 1)
            parts = stacked.reshape((high, 2, 1 << b) + shape[1:])
            stacked = jnp.where(odd, parts[:, ::-1], parts).reshape(shape)
        return stacked

    def scatter_dp(self, grad):
        m, n, w = grad.shape
        r = n // self.pieces
        parts = grad.astype(BF16).reshape((m,) + (2,) * self.low + (r, w))

        def halve(now, b):
            axis = 1 + self.low - 1 - b
            mine = self.bit(b)
            keep = lax.dynamic_slice_in_dim(now, mine, 1, axis)
            send = lax.dynamic_slice_in_dim(now, 1 - mine, 1, axis)
            got = self.pair(send, b)
            return (keep.astype(F32) + got.astype(F32)).astype(BF16)

        now = halve(parts, 0)
        halves = []
        rows_axis = 1 + self.low
        for order, part in zip(self.orders(), jnp.split(now, 2, axis=rows_axis)):
            for b in order:
                part = halve(part, b)
            halves.append(part.reshape(m, r // 2, w))
        return jnp.concatenate(halves, 1)

    def reduce_grad(self, grad):
        piece = self.scatter_dp(grad)
        total = lax.dynamic_index_in_dim(piece, self.mp, 0, keepdims=False).astype(F32)
        for j in range(1, self.nmp):
            send = lax.dynamic_index_in_dim(piece, self.mp ^ j, 0, keepdims=False)
            total = total + self.across(send, j).astype(F32)
        for b in range(self.low, self.bits):
            total = total + self.pair(total.astype(BF16), b).astype(F32)
        out = self.gather_dp(total.astype(BF16)[None])[0]
        return out.astype(F32)


def body(
    inputs,
    lengths,
    ln1_gain,
    ln1_bias,
    w_qkv,
    b_qkv,
    w_out,
    b_out,
    ln2_gain,
    ln2_bias,
    w_up,
    b_up,
    w_down,
    b_down,
    cotangent,
):
    net = Links()
    row_count, local_len, width = inputs.shape
    nmp = net.nmp
    heads = width // HDIM
    core = net.dp % 2
    z = net.mp
    other = net.pair(lengths, 0)
    four = jnp.where(core == 1, jnp.concatenate([other, lengths]), jnp.concatenate([lengths, other]))
    length = lax.dynamic_index_in_dim(four, z, 0, keepdims=False)

    def positions_of(c):
        blocks = [
            (2 * c + ((z % 2) ^ k)) * local_len + jnp.arange(local_len, dtype=jnp.int32)
            for k in range(2)
        ]
        return jnp.concatenate(blocks)

    pos_here = positions_of(core)
    pos_all = jnp.concatenate([pos_here, positions_of(1 - core)])
    keep = (pos_here < length).astype(F32)[:, None]
    key_keep = pos_all < length
    cosine, sine_table = rotary_tables(pos_here, HDIM)

    x_blocks = net.to_rows(inputs)
    lw = w_qkv.shape[2]
    w_qkv_t = jnp.swapaxes(w_qkv, 1, 2).reshape(3 * lw, width)
    wq_all = net.gather_weight(jnp.concatenate([w_qkv_t, w_out], 0))
    wq = wq_all[:, : 3 * lw].reshape(nmp, 3, lw, width)
    wo = wq_all[:, 3 * lw :].reshape(nmp * lw, width)
    small = jnp.concatenate([b_qkv.reshape(-1), b_up.astype(F32)])
    small_all = net.by_mp([small] + [net.across(small, j) for j in range(1, nmp)])
    bq_all = small_all[:, : 3 * lw].reshape(nmp, 3, lw)
    bu_all = small_all[:, 3 * lw :]
    wu = net.gather_weight(w_up)
    wd = net.gather_weight(w_down)
    g_blocks = net.to_rows(cotangent)

    x = jnp.concatenate(x_blocks).astype(F32)
    n_tok = x.shape[0]
    unit1, scale1 = norm_stats(x)
    normed_one = (unit1 * ln1_gain + ln1_bias).astype(BF16)
    qkv = jnp.einsum("ld,mted->ltme", normed_one, wq, preferred_element_type=F32)
    qkv = qkv + jnp.swapaxes(bq_all, 0, 1)[None]
    qkv = qkv.reshape(n_tok, 3, heads, HDIM)
    q = rotate(qkv[:, 0], cosine, sine_table).astype(BF16)
    k = rotate(qkv[:, 1], cosine, sine_table).astype(BF16)
    v = qkv[:, 2].astype(BF16)
    k_other = net.pair(k, 0)
    v_other = net.pair(v, 0)
    k_all = jnp.concatenate([k, k_other])
    v_all = jnp.concatenate([v, v_other])
    att_scale = HDIM ** (-0.5)
    scores = jnp.einsum("qhe,khe->hqk", q, k_all, preferred_element_type=F32) * att_scale
    scores = jnp.where(key_keep[None, None, :], scores, masked_score)
    row_max = jnp.max(scores, -1, keepdims=True)
    weights = jnp.exp(scores - row_max)
    probs = (weights / jnp.sum(weights, -1, keepdims=True)).astype(BF16)
    mixed = jnp.einsum("hqk,khe->qhe", probs, v_all, preferred_element_type=F32)
    mixed = mixed.astype(BF16).reshape(n_tok, width)
    residual = x + (jnp.dot(mixed, wo, preferred_element_type=F32) + b_out)
    unit2, scale2 = norm_stats(residual)
    normed_two = (unit2 * ln2_gain + ln2_bias).astype(BF16)
    up = jnp.einsum("ld,mdf->lmf", normed_two, wu, preferred_element_type=F32) + bu_all
    act = jax.nn.gelu(up, approximate=False).astype(BF16)
    down = jnp.einsum("lmf,mfd->ld", act, wd, preferred_element_type=F32) + b_down
    layer_rows = ((residual + down) * keep).astype(BF16)
    layer_out = net.from_rows([layer_rows[:local_len], layer_rows[local_len:]])

    grad_down = jnp.concatenate(g_blocks).astype(F32) * keep
    grad_down_low = grad_down.astype(BF16)
    grad_b_down = jnp.sum(grad_down, 0)
    grad_w_down = jnp.einsum("lmf,ld->mfd", act, grad_down_low, preferred_element_type=F32)
    grad_act = jnp.einsum("ld,mfd->lmf", grad_down_low, wd, preferred_element_type=F32)
    grad_up = (grad_act * gelu_slope(up)).astype(BF16)
    grad_b_up = jnp.sum(grad_up, 0, dtype=F32)
    grad_w_up = jnp.einsum("ld,lmf->mdf", normed_two, grad_up, preferred_element_type=F32)
    grad_normed_two = jnp.einsum("lmf,mdf->ld", grad_up, wu, preferred_element_type=F32)
    grad_ln2_gain = jnp.sum(grad_normed_two * unit2, 0)
    grad_ln2_bias = jnp.sum(grad_normed_two, 0)
    grad_residual = grad_down + norm_back(grad_normed_two, unit2, scale2, ln2_gain)
    grad_w_down = net.reduce_grad(grad_w_down)
    grad_w_up = net.reduce_grad(grad_w_up)

    grad_attn = grad_residual.astype(BF16)
    grad_b_out = jnp.sum(grad_attn, 0, dtype=F32)
    grad_w_out = jnp.dot(mixed.T, grad_attn, preferred_element_type=F32)
    grad_mixed = jnp.einsum("ld,cd->lc", grad_attn, wo, preferred_element_type=F32).astype(BF16)
    inner_sum = jnp.sum(
        (grad_mixed.astype(F32) * mixed.astype(F32)).reshape(n_tok, heads, HDIM), -1
    )
    grad_mixed = grad_mixed.reshape(n_tok, heads, HDIM)
    grad_probs = jnp.einsum("qhe,khe->hqk", grad_mixed, v_all, preferred_element_type=F32)
    grad_scores = (probs.astype(F32) * (grad_probs - inner_sum.T[:, :, None])).astype(BF16)
    grad_v = jnp.einsum("hqk,qhe->khe", probs, grad_mixed, preferred_element_type=F32)
    grad_q = jnp.einsum("hqk,khe->qhe", grad_scores, k_all, preferred_element_type=F32) * att_scale
    grad_k = jnp.einsum("hqk,qhe->khe", grad_scores, q, preferred_element_type=F32) * att_scale
    grad_k = grad_k[:n_tok] + net.pair(grad_k[n_tok:].astype(BF16), 0).astype(F32)
    grad_v = grad_v[:n_tok] + net.pair(grad_v[n_tok:].astype(BF16), 0).astype(F32)
    grad_qkv = jnp.stack(
        [
            rotate_back(grad_q, cosine, sine_table),
            rotate_back(grad_k, cosine, sine_table),
            grad_v,
        ],
        1,
    )
    grad_qkv = grad_qkv.astype(BF16).reshape(n_tok, 3, nmp, lw)
    grad_b_qkv = jnp.sum(grad_qkv, 0, dtype=F32)
    grad_w_qkv = jnp.einsum("ltme,ld->mted", grad_qkv, normed_one, preferred_element_type=F32)
    first = jnp.einsum("ltme,mted->ld", grad_qkv, wq, preferred_element_type=F32)
    grad_ln1_gain = jnp.sum(first * unit1, 0)
    grad_ln1_bias = jnp.sum(first, 0)
    grad_x = (grad_residual + norm_back(first, unit1, scale1, ln1_gain)).astype(BF16)
    grad_inputs = net.from_rows([grad_x[:local_len], grad_x[local_len:]]).astype(F32)
    packed = net.reduce_grad(
        jnp.concatenate(
            [grad_w_qkv.reshape(nmp, 3 * lw, width), grad_w_out.reshape(nmp, lw, width)], 1
        )
    )
    grad_w_qkv = jnp.swapaxes(packed[: 3 * lw].reshape(3, lw, width), 1, 2)
    grad_w_out = packed[3 * lw :]

    vec = jnp.concatenate(
        [
            grad_ln1_gain,
            grad_ln1_bias,
            grad_b_out,
            grad_ln2_gain,
            grad_ln2_bias,
            grad_b_down,
            jnp.swapaxes(grad_b_qkv, 0, 1).reshape(-1),
            grad_b_up.reshape(-1),
        ]
    )
    vec = lax.psum(vec, ("dp", "mp"))
    reps = [vec[i * width : (i + 1) * width] for i in range(6)]
    rest = vec[6 * width :]
    bq = rest[: 3 * nmp * lw].reshape(nmp, 3, lw)
    bu = rest[3 * nmp * lw :].reshape(nmp, -1)
    grad_b_qkv = lax.dynamic_index_in_dim(bq, z, 0, keepdims=False)
    grad_b_up = lax.dynamic_index_in_dim(bu, z, 0, keepdims=False)
    return (
        layer_out,
        grad_inputs,
        reps[0],
        reps[1],
        grad_w_qkv,
        grad_b_qkv,
        grad_w_out,
        reps[2],
        reps[3],
        reps[4],
        grad_w_up,
        grad_b_up,
        grad_w_down,
        reps[5],
    )


def solution(mesh):
    return jax.shard_map(
        body,
        mesh=mesh,
        in_specs=(
            P("dp", "mp", None),
            P("dp"),
            P(),
            P(),
            P(None, None, "mp"),
            P(None, "mp"),
            P("mp", None),
            P(),
            P(),
            P(),
            P(None, "mp"),
            P("mp"),
            P("mp", None),
            P(),
            P("dp", "mp", None),
        ),
        out_specs=(
            P("dp", "mp", None),
            P("dp", "mp", None),
            P(),
            P(),
            P(None, None, "mp"),
            P(None, "mp"),
            P("mp", None),
            P(),
            P(),
            P(),
            P(None, "mp"),
            P("mp"),
            P("mp", None),
            P(),
        ),
        check_vma=False,
    )
```

```python
import functools
import math

import jax
import jax.numpy as jnp
from jax import lax
from jax.experimental import pallas as pl
from jax.experimental.pallas import tpu as pltpu
from jax.sharding import PartitionSpec as P

HDIM = 64
norm_eps = 1e-05
masked_score = -1000000000.0
F32 = jnp.float32
BF16 = jnp.bfloat16
MESH = pl.DeviceIdType.MESH
NT = (((1,), (1,)), ((), ()))
NN = (((1,), (0,)), ((), ()))
TN = (((0,), (0,)), ((), ()))
ANY = pl.BlockSpec(memory_space=pl.ANY)
VMEM = pl.BlockSpec(memory_space=pltpu.VMEM)


def dot(a, b, form):
    return lax.dot_general(a, b, form, preferred_element_type=F32)


def lanes(i):
    return pl.ds(pl.multiple_of(i * 128, 128), 128)


class Place:
    def __init__(self):
        self.dp = lax.axis_index("dp")
        self.z = lax.axis_index("mp")
        self.b0 = self.dp % 2
        self.b1 = (self.dp // 2) % 2
        self.b2 = (self.dp // 4) % 2
        dp, z = self.dp, self.z
        self.core = (dp + 1 - 2 * self.b0, z)
        self.d1 = (dp + 2 - 4 * self.b1, z)
        self.d2 = (dp + 4 - 8 * self.b2, z)
        self.z1 = (dp, z + 1 - 2 * (z % 2))
        self.z2 = (dp, z + 2 - 4 * (z // 2))
        base = dp - self.b0 + z // 2
        self.row0 = (base, 2 * self.b0 + z % 2)
        self.row1 = (base, 2 * self.b0 + 1 - z % 2)
        self.stays = self.b0 == z // 2

    def greet(self, row_partners):
        barrier = pltpu.get_barrier_semaphore()
        peers = [self.core, self.d1, self.d2, self.z1, self.z2]
        if row_partners:
            peers.append(self.row1)
        for peer in peers:
            pl.semaphore_signal(barrier, inc=1, device_id=peer, device_id_type=MESH)
        count = len(peers)
        if row_partners:
            moves = jnp.where(self.stays, 0, 1)
            count = count + moves

            @pl.when(moves == 1)
            def _():
                pl.semaphore_signal(barrier, inc=1, device_id=self.row0, device_id_type=MESH)

        pl.semaphore_wait(barrier, count)


class Sender:
    def __init__(self, send_sems, recv_sems):
        self.send_sems, self.recv_sems = send_sems, recv_sems
        self.used = 0
        self.sent = []

    def remote(self, src, dst, peer):
        i = self.used
        self.used += 1
        copy = pltpu.make_async_remote_copy(
            src_ref=src,
            dst_ref=dst,
            send_sem=self.send_sems.at[i],
            recv_sem=self.recv_sems.at[i],
            device_id=peer,
            device_id_type=MESH,
        )
        copy.start()
        self.sent.append(copy)
        return copy

    def local(self, src, dst):
        i = self.used
        self.used += 1
        copy = pltpu.make_async_copy(src, dst, self.recv_sems.at[i])
        copy.start()
        return copy

    def finish(self):
        for copy in self.sent:
            copy.wait_send()


class RowMove:
    def __init__(self, here, sender, src0, src1, dst):
        self.here, self.sender = here, sender
        i = sender.used
        sender.used += 1
        self.keep = pltpu.make_async_copy(src0, dst, sender.recv_sems.at[i])
        self.first = pltpu.make_async_remote_copy(
            src_ref=src0,
            dst_ref=dst,
            send_sem=sender.send_sems.at[i],
            recv_sem=sender.recv_sems.at[i],
            device_id=here.row0,
            device_id_type=MESH,
        )

        @pl.when(here.stays)
        def _():
            self.keep.start()

        @pl.when(jnp.logical_not(here.stays))
        def _():
            self.first.start()

        self.second = sender.remote(src1, dst, here.row1)

    def wait(self):
        @pl.when(self.here.stays)
        def _():
            self.keep.wait()

        @pl.when(jnp.logical_not(self.here.stays))
        def _():
            self.first.wait()

        self.second.wait_recv()


class Gather:
    def __init__(self, here, sender, own, ref):
        self.here, self.sender, self.own, self.ref = here, sender, own, ref
        n = ref.shape[1]
        self.half = n // 2
        self.eighth = n // 8
        self.piece = n // 16
        h = here
        start = h.b0 * self.half
        self.rows = [
            start + h.b2 * self.eighth + h.b1 * self.piece,
            start + self.half // 2 + h.b1 * self.eighth + h.b2 * self.piece,
        ]
        self.pairs = [start + h.b2 * self.eighth, start + self.half // 2 + h.b1 * self.eighth]
        self.flying = []

    def ds(self, start, size):
        return pl.ds(pl.multiple_of(start, 16), size)

    def land(self):
        for copy in self.flying:
            copy.wait_recv()
        self.flying = []

    def begin(self):
        for r in self.rows:
            at = self.ds(r, self.piece)
            self.flying.append(
                self.sender.remote(self.own.at[at], self.ref.at[1, at], self.here.z2)
            )

    def step_z1(self):
        for r in self.rows:
            at = self.ds(r, self.piece)
            self.flying.append(
                self.sender.remote(self.own.at[at], self.ref.at[2, at], self.here.z1)
            )
        first, self.flying = self.flying[:2], self.flying[2:]
        for copy in first:
            copy.wait_recv()
        for r in self.rows:
            at = self.ds(r, self.piece)
            self.flying.append(
                self.sender.remote(self.ref.at[1, at], self.ref.at[3, at], self.here.z1)
            )

    def spread(self, at, peer):
        view = self.ref.at[pl.ds(1, 3), at]
        self.flying.append(self.sender.remote(view, view, peer))

    def step_d1(self):
        self.land()
        self.spread(self.ds(self.rows[0], self.piece), self.here.d1)
        self.spread(self.ds(self.rows[1], self.piece), self.here.d2)

    def step_d2(self):
        self.land()
        self.spread(self.ds(self.pairs[0], self.eighth), self.here.d2)
        self.spread(self.ds(self.pairs[1], self.eighth), self.here.d1)

    def step_core(self):
        self.land()
        self.spread(self.ds(self.here.b0 * self.half, self.half), self.here.core)


def normalize(values):
    middle = jnp.mean(values, axis=-1, keepdims=True)
    centred = values - middle
    spread = jnp.mean(centred * centred, axis=-1, keepdims=True)
    scale = lax.rsqrt(spread + norm_eps)
    return centred * scale, scale


def low_half():
    return lax.broadcasted_iota(jnp.int32, (1, 128), 1) % 64 < 32


def rotate_lanes(values, cosine, signed_sine):
    turned = jnp.where(low_half(), pltpu.roll(values, 96, 1), pltpu.roll(values, 32, 1))
    return values * cosine + turned * signed_sine


def first_kernel(
    inputs,
    cotangent,
    lens,
    own_one,
    own_up,
    own_down,
    small,
    vectors,
    x_out,
    n1_out,
    q_out,
    k_out,
    v_out,
    p_out,
    mixed_out,
    res_out,
    n2_out,
    w1_out,
    up_out,
    down_out,
    small_out,
    cot_out,
    len_out,
    xbuf,
    n1,
    q,
    k_all,
    v_all,
    probs,
    mixed,
    res,
    n2,
    w1,
    smalls,
    length_ref,
    cots,
    cosine,
    sine,
    send_sems,
    recv_sems,
):
    here = Place()
    net = Sender(send_sems, recv_sems)
    n_tok, width = n1.shape
    half_tok = n_tok // 2
    total = k_all.shape[0]
    lw = (w1.shape[1] * 3 // 4) // 3
    c, z = here.b0, here.z
    with jax.named_scope("greet"):
        here.greet(True)
    one = Gather(here, net, own_one, w1)
    up = Gather(here, net, own_up, up_out)
    down = Gather(here, net, own_down, down_out)
    one.begin()
    own_copy = net.local(own_one, w1.at[0])
    slot = z % 2
    arrive_x = RowMove(
        here, net, inputs.at[z % 2], inputs.at[1 - z % 2], xbuf.at[slot]
    )
    arrive_len = net.remote(lens.at[1 - z % 2], length_ref, here.row1)
    small_own = net.local(small, smalls.at[0])
    small_a = net.remote(small, smalls.at[1], here.z2)

    lane = lax.broadcasted_iota(jnp.int32, (1, 128), 1)
    frequency = jnp.exp((lane % 32).astype(F32) * (-2.0 * math.log(10000.0) / HDIM))

    def tables(i, carry):
        at = pl.ds(pl.multiple_of(i * 64, 64), 64)
        place = c * n_tok + i * 64 + lax.broadcasted_iota(jnp.int32, (64, 1), 0)
        angles = place.astype(F32) * frequency
        cosine[at, :] = jnp.cos(angles)
        sine[at, :] = jnp.where(low_half(), -1.0, 1.0) * jnp.sin(angles)
        return carry

    with jax.named_scope("tables"):
        lax.fori_loop(0, n_tok // 64, tables, 0)

    with jax.named_scope("one_z1"):
        one.step_z1()
    small_own.wait()
    small_a.wait_recv()
    small_b = net.remote(smalls.at[pl.ds(0, 2)], smalls.at[pl.ds(2, 2)], here.z1)
    with jax.named_scope("one_d1"):
        one.step_d1()
    up.begin()
    down.begin()
    with jax.named_scope("one_d2"):
        one.step_d2()
    with jax.named_scope("wait_x"):
        arrive_x.wait()
    x_copy = net.local(xbuf, x_out)

    def norm_one(i, carry):
        for b in range(2):
            at = pl.ds(pl.multiple_of(i * 64, 64), 64)
            unit, _ = normalize(xbuf[b, at, :].astype(F32))
            to = pl.ds(pl.multiple_of(b * half_tok + i * 64, 64), 64)
            n1[to, :] = (unit * vectors[0:1, :] + vectors[1:2, :]).astype(BF16)
        return carry

    with jax.named_scope("norm_one"):
        lax.fori_loop(0, half_tok // 64, norm_one, 0)
    n1_copy = net.local(n1, n1_out)
    with jax.named_scope("one_core"):
        one.step_core()
    with jax.named_scope("ud_z1"):
        up.step_z1()
        down.step_z1()
    small_b.wait_recv()
    with jax.named_scope("one_land"):
        one.land()
        own_copy.wait()
    w1_copy = net.local(w1, w1_out)
    mine = pl.ds(pl.multiple_of(c * n_tok, n_tok), n_tok)

    def bias_of(t):
        rest = lw - 128
        parts = []
        for s in range(4):
            parts.append(smalls[s, 2 * t : 2 * t + 1, :])
            parts.append(smalls[s, 2 * t + 1 : 2 * t + 2, 0:rest])
        return jnp.concatenate(parts, 1)

    def qkv_of(t):
        rows = jnp.concatenate([w1[s, t * lw : (t + 1) * lw, :] for s in range(4)], 0)
        return dot(n1[...], rows, NT) + bias_of(t)

    with jax.named_scope("proj_k"):
        raw = qkv_of(1)
    for i in range(width // 128):
        part = raw[:, i * 128 : (i + 1) * 128]
        k_all[mine, i * 128 : (i + 1) * 128] = rotate_lanes(
            part, cosine[...], sine[...]
        ).astype(BF16)
    move_k = net.remote(k_all.at[mine], k_all.at[mine], here.core)
    with jax.named_scope("proj_v"):
        v_all[mine, :] = qkv_of(2).astype(BF16)
    move_v = net.remote(v_all.at[mine], v_all.at[mine], here.core)
    with jax.named_scope("ud_d1"):
        up.step_d1()
        down.step_d1()
    arrive_cot = RowMove(
        here, net, cotangent.at[z % 2], cotangent.at[1 - z % 2], cots.at[slot]
    )
    raw = qkv_of(0)
    for i in range(width // 128):
        part = raw[:, i * 128 : (i + 1) * 128]
        turned = rotate_lanes(part, cosine[...], sine[...]).astype(BF16)
        q[:, i * 128 : (i + 1) * 128] = turned * jnp.asarray(HDIM**-0.5, BF16)
    q_copy = net.local(q, q_out)
    with jax.named_scope("wait_kv"):
        move_k.wait_recv()
        move_v.wait_recv()
    k_copy = net.local(k_all, k_out)
    v_copy = net.local(v_all, v_out)
    arrive_len.wait_recv()
    len_copy = net.local(length_ref, len_out)
    small_copy = net.local(smalls, small_out)

    tile = 256
    first_lanes = lax.broadcasted_iota(jnp.int32, (1, 128), 1) < HDIM
    p_sem = net.used
    net.used += 2

    def p_move(i, s):
        return pltpu.make_async_copy(
            probs.at[s], p_out.at[pl.ds(2 * i, 2)], recv_sems.at[p_sem + s]
        )

    def pair(i, carry):
        s = i % 2

        @pl.when(i >= 2)
        def _():
            p_move(i - 2, s).wait()

        key_place = lax.broadcasted_iota(jnp.int32, (1, total), 1).astype(F32)
        mask = key_place < length_ref[0:1, 0:1]
        kp = k_all[:, lanes(i)]
        vp = v_all[:, lanes(i)]
        for t in range(n_tok // tile):
            at = pl.ds(t * tile, tile)
            sums = 0.0
            for h in range(2):
                chosen = first_lanes if h == 0 else jnp.logical_not(first_lanes)
                kh = jnp.where(chosen, kp, 0)
                vh = jnp.where(chosen, vp, 0)
                scores = jnp.where(mask, dot(q[at, lanes(i)], kh, NT), masked_score)
                top = jnp.max(scores, 1, keepdims=True)
                weights = jnp.exp(scores - top)
                part = (weights * (1.0 / jnp.sum(weights, 1, keepdims=True))).astype(BF16)
                probs[s, h, at, :] = part
                sums = sums + dot(part, vh, NN)
            mixed[at, lanes(i)] = sums.astype(BF16)
        p_move(i, s).start()
        return carry

    pairs = width // 128
    with jax.named_scope("attend_a"):
        lax.fori_loop(0, 2, pair, 0)
    with jax.named_scope("up_d2"):
        up.step_d2()
    with jax.named_scope("attend_b"):
        lax.fori_loop(2, 3, pair, 0)
    with jax.named_scope("down_d2"):
        down.step_d2()
    with jax.named_scope("attend_c"):
        lax.fori_loop(3, 5, pair, 0)
    with jax.named_scope("up_core"):
        up.step_core()
    with jax.named_scope("attend_d"):
        lax.fori_loop(5, pairs, pair, 0)
    mixed_copy = net.local(mixed, mixed_out)
    wo = jnp.concatenate([w1[s, 3 * lw : 4 * lw, :] for s in range(4)], 0)
    with jax.named_scope("project_out"):
        res[...] = dot(mixed[...], wo, NN)

    def norm_two(i, carry):
        for b in range(2):
            at = pl.ds(pl.multiple_of(i * 64, 64), 64)
            to = pl.ds(pl.multiple_of(b * half_tok + i * 64, 64), 64)
            value = xbuf[b, at, :].astype(F32) + (res[to, :] + vectors[2:3, :])
            res[to, :] = value
            unit, _ = normalize(value)
            n2[to, :] = (unit * vectors[3:4, :] + vectors[4:5, :]).astype(BF16)
        return carry

    with jax.named_scope("norm_two"):
        lax.fori_loop(0, half_tok // 64, norm_two, 0)
    with jax.named_scope("down_core"):
        down.step_core()
    copies = [net.local(res, res_out), net.local(n2, n2_out)]
    for i in range(pairs - 2, pairs):
        p_move(i, i % 2).wait()
    copies += [x_copy, n1_copy, w1_copy, q_copy, k_copy, v_copy, len_copy, small_copy, mixed_copy]
    with jax.named_scope("last_waits"):
        for copy in copies:
            copy.wait()
        arrive_cot.wait()
        cot_copy = net.local(cots, cot_out)
        up.land()
        down.land()
        net.finish()
        cot_copy.wait()


def first_part(inputs, cotangent, lengths, own_one, w_up, w_down, small, vectors):
    _, local_len, width = inputs.shape
    n_tok = 2 * local_len
    total = 4 * local_len
    heads = width // HDIM
    n = own_one.shape[0]
    lens = jnp.broadcast_to(lengths.astype(F32)[:, None, None], (2, 8, 128))
    sds = jax.ShapeDtypeStruct
    outs = (
        sds((2, local_len, width), BF16),
        sds((n_tok, width), BF16),
        sds((n_tok, width), BF16),
        sds((total, width), BF16),
        sds((total, width), BF16),
        sds((heads, n_tok, total), BF16),
        sds((n_tok, width), BF16),
        sds((n_tok, width), F32),
        sds((n_tok, width), BF16),
        sds((4, n, width), BF16),
        sds((4,) + w_up.shape, BF16),
        sds((4,) + w_down.shape, BF16),
        sds((4,) + small.shape, F32),
        sds((2, local_len, width), BF16),
        sds((8, 128), F32),
    )
    scratch = [
        pltpu.VMEM((2, local_len, width), BF16),
        pltpu.VMEM((n_tok, width), BF16),
        pltpu.VMEM((n_tok, width), BF16),
        pltpu.VMEM((total, width), BF16),
        pltpu.VMEM((total, width), BF16),
        pltpu.VMEM((2, 2, n_tok, total), BF16),
        pltpu.VMEM((n_tok, width), BF16),
        pltpu.VMEM((n_tok, width), F32),
        pltpu.VMEM((n_tok, width), BF16),
        pltpu.VMEM((4, n, width), BF16),
        pltpu.VMEM((4,) + small.shape, F32),
        pltpu.VMEM((8, 128), F32),
        pltpu.VMEM((2, local_len, width), BF16),
        pltpu.VMEM((n_tok, 128), F32),
        pltpu.VMEM((n_tok, 128), F32),
        pltpu.SemaphoreType.DMA((64,)),
        pltpu.SemaphoreType.DMA((64,)),
    ]
    return pl.pallas_call(
        first_kernel,
        out_shape=outs,
        in_specs=[ANY] * 7 + [VMEM],
        out_specs=[ANY] * len(outs),
        scratch_shapes=scratch,
        compiler_params=pltpu.CompilerParams(
            collective_id=1, has_side_effects=True, vmem_limit_bytes=56 * 2**20
        ),
        name="forward_attention",
    )(inputs, cotangent, lens, own_one, w_up, w_down, small, vectors)


def rotary_tables(positions, head_size):
    freq_steps = jnp.arange(head_size // 2, dtype=F32)
    frequency = jnp.exp(freq_steps * (-2.0 * math.log(10000.0) / head_size))
    angles = positions.astype(F32)[:, None] * frequency[None, :]
    cosine = jnp.concatenate([jnp.cos(angles), jnp.cos(angles)], -1)
    sine_table = jnp.concatenate([jnp.sin(angles), jnp.sin(angles)], -1)
    return (cosine, sine_table)


def rotate_back(grads_in, cosine, sine_table):
    half_size = grads_in.shape[-1] // 2
    scaled = grads_in * sine_table[:, None, :]
    turned = jnp.concatenate([scaled[..., half_size:], -scaled[..., :half_size]], -1)
    return grads_in * cosine[:, None, :] + turned


def gelu_slope(values):
    return (
        0.5 * (1.0 + lax.erf(values * 0.7071067811865476))
        + values * jnp.exp(-0.5 * values * values) * 0.3989422804014327
    )


def norm_stats(values):
    middle = jnp.mean(values, axis=-1, keepdims=True)
    centred = values - middle
    spread = jnp.mean(centred * centred, axis=-1, keepdims=True)
    scale = lax.rsqrt(spread + norm_eps)
    return centred * scale, scale


def norm_back(grad, unit, scale, gain):
    h = grad * gain
    return scale * (
        h
        - jnp.mean(h, axis=-1, keepdims=True)
        - unit * jnp.mean(h * unit, axis=-1, keepdims=True)
    )


class Links:
    def __init__(self):
        self.ndp = lax.axis_size("dp")
        self.nmp = lax.axis_size("mp")
        self.dp = lax.axis_index("dp")
        self.mp = lax.axis_index("mp")
        self.bits = self.ndp.bit_length() - 1
        self.low = min(3, self.bits)
        self.pieces = 1 << self.low

    def bit(self, b):
        return (self.dp >> b) & 1

    def pair(self, x, b):
        return lax.ppermute(x, "dp", [(i, i ^ (1 << b)) for i in range(self.ndp)])

    def across(self, x, j):
        return lax.ppermute(x, "mp", [(i, i ^ j) for i in range(self.nmp)])

    def row_perm(self, k, back):
        pairs = []
        for dp in range(self.ndp):
            for z in range(self.nmp):
                q, c = dp // 2, dp % 2
                src = dp * self.nmp + z
                dst = (2 * q + z // 2) * self.nmp + 2 * c + ((z % 2) ^ k)
                pairs.append((dst, src) if back else (src, dst))
        return pairs

    def from_rows(self, blocks):
        odd = self.mp % 2 == 1
        blocks = [jnp.where(odd, blocks[1], blocks[0]), jnp.where(odd, blocks[0], blocks[1])]
        got = [
            lax.ppermute(blocks[k], ("dp", "mp"), self.row_perm(k, True)) for k in range(2)
        ]
        return jnp.stack([jnp.where(odd, got[1], got[0]), jnp.where(odd, got[0], got[1])])

    def join(self, own, other, b, axis):
        return jnp.where(
            self.bit(b) == 1,
            jnp.concatenate([other, own], axis),
            jnp.concatenate([own, other], axis),
        )

    def orders(self):
        upper = list(range(1, self.low))
        return [upper, upper[::-1]]

    def gather_dp(self, piece):
        k, r, w = piece.shape
        halves = []
        for order, half in zip(self.orders(), (piece[:, : r // 2], piece[:, r // 2 :])):
            now = half.reshape((k,) + (1,) * self.low + (r // 2, w))
            for b in order + [0]:
                now = self.join(now, self.pair(now, b), b, 1 + self.low - 1 - b)
            halves.append(now)
        whole = jnp.concatenate(halves, axis=1 + self.low)
        return whole.reshape(k, self.pieces * r, w)

    def by_mp(self, items):
        stacked = jnp.stack(items)
        for b in range(self.nmp.bit_length() - 1):
            odd = ((self.mp >> b) & 1) == 1
            shape = stacked.shape
            high = self.nmp >> (b + 1)
            parts = stacked.reshape((high, 2, 1 << b) + shape[1:])
            stacked = jnp.where(odd, parts[:, ::-1], parts).reshape(shape)
        return stacked

    def scatter_dp(self, grad):
        m, n, w = grad.shape
        r = n // self.pieces
        parts = grad.astype(BF16).reshape((m,) + (2,) * self.low + (r, w))

        def halve(now, b):
            axis = 1 + self.low - 1 - b
            mine = self.bit(b)
            keep = lax.dynamic_slice_in_dim(now, mine, 1, axis)
            send = lax.dynamic_slice_in_dim(now, 1 - mine, 1, axis)
            got = self.pair(send, b)
            return (keep.astype(F32) + got.astype(F32)).astype(BF16)

        now = halve(parts, 0)
        halves = []
        rows_axis = 1 + self.low
        for order, part in zip(self.orders(), jnp.split(now, 2, axis=rows_axis)):
            for b in order:
                part = halve(part, b)
            halves.append(part.reshape(m, r // 2, w))
        return jnp.concatenate(halves, 1)

    def reduce_grad(self, grad):
        piece = self.scatter_dp(grad)
        piece = piece.astype(F32)
        piece = piece[:2] + self.across(piece[2:].astype(BF16), 1).astype(F32)
        total = piece[0] + self.across(piece[1].astype(BF16), 2).astype(F32)
        for b in range(self.low, self.bits):
            total = total + self.pair(total.astype(BF16), b).astype(F32)
        out = self.gather_dp(total.astype(BF16)[None])[0]
        return out.astype(F32)


def body(
    inputs,
    lengths,
    ln1_gain,
    ln1_bias,
    w_qkv,
    b_qkv,
    w_out,
    b_out,
    ln2_gain,
    ln2_bias,
    w_up,
    b_up,
    w_down,
    b_down,
    cotangent,
):
    net = Links()
    row_count, local_len, width = inputs.shape
    nmp = net.nmp
    heads = width // HDIM
    core = net.dp % 2
    z = net.mp
    lw = w_qkv.shape[2]
    w_qkv_t = jnp.swapaxes(w_qkv, 1, 2).reshape(3 * lw, width)
    own_one = jnp.concatenate([w_qkv_t, w_out], 0)
    small = jnp.concatenate(
        [
            jnp.pad(b_qkv, ((0, 0), (0, 256 - lw))).reshape(6, 128),
            jnp.zeros((2, 128), F32),
            b_up.astype(F32).reshape(-1, 128),
            jnp.zeros((2, 128), F32),
        ]
    )
    vectors = jnp.stack([ln1_gain, ln1_bias, b_out, ln2_gain, ln2_bias, b_down, b_down, b_down])
    (
        x_blocks,
        normed_one,
        q,
        k_all,
        v_all,
        probs,
        mixed,
        residual,
        normed_two,
        wq_all,
        wu,
        wd,
        small_all,
        g_blocks,
        len_all,
    ) = first_part(inputs, cotangent, lengths, own_one, w_up, w_down, small, vectors)
    wq = wq_all[:, : 3 * lw].reshape(nmp, 3, lw, width)
    wo = wq_all[:, 3 * lw :].reshape(nmp * lw, width)
    wu = jnp.concatenate([w_up[None], wu[1:]])
    wd = jnp.concatenate([w_down[None], wd[1:]])
    bu_all = small_all[:, 8:14].reshape(nmp, -1)
    n_tok = 2 * local_len
    pos_here = core * n_tok + jnp.arange(n_tok, dtype=jnp.int32)
    keep = (pos_here.astype(F32) < len_all[0, 0]).astype(F32)[:, None]
    cosine, sine_table = rotary_tables(pos_here, HDIM)
    x = x_blocks.reshape(n_tok, width).astype(F32)
    unit1, scale1 = norm_stats(x)
    att_scale = HDIM ** (-0.5)
    q = q.reshape(n_tok, heads, HDIM)
    k_all = k_all.reshape(2 * n_tok, heads, HDIM)
    v_all = v_all.reshape(2 * n_tok, heads, HDIM)
    unit2, scale2 = norm_stats(residual)
    up = jnp.einsum("ld,mdf->lmf", normed_two, wu, preferred_element_type=F32) + bu_all
    act = jax.nn.gelu(up, approximate=False).astype(BF16)
    down = jnp.einsum("lmf,mfd->ld", act, wd, preferred_element_type=F32) + b_down
    layer_rows = ((residual + down) * keep).astype(BF16)
    layer_out = net.from_rows([layer_rows[:local_len], layer_rows[local_len:]])

    grad_down = g_blocks.reshape(n_tok, width).astype(F32) * keep
    grad_down_low = grad_down.astype(BF16)
    grad_b_down = jnp.sum(grad_down, 0)
    grad_w_down = jnp.einsum("lmf,ld->mfd", act, grad_down_low, preferred_element_type=F32)
    grad_act = jnp.einsum("ld,mfd->lmf", grad_down_low, wd, preferred_element_type=F32)
    grad_up = (grad_act * gelu_slope(up)).astype(BF16)
    grad_b_up = jnp.sum(grad_up, 0, dtype=F32)
    grad_w_up = jnp.einsum("ld,lmf->mdf", normed_two, grad_up, preferred_element_type=F32)
    grad_normed_two = jnp.einsum("lmf,mdf->ld", grad_up, wu, preferred_element_type=F32)
    grad_ln2_gain = jnp.sum(grad_normed_two * unit2, 0)
    grad_ln2_bias = jnp.sum(grad_normed_two, 0)
    grad_residual = grad_down + norm_back(grad_normed_two, unit2, scale2, ln2_gain)
    grad_w_down = net.reduce_grad(grad_w_down)
    grad_w_up = net.reduce_grad(grad_w_up)

    grad_attn = grad_residual.astype(BF16)
    grad_b_out = jnp.sum(grad_attn, 0, dtype=F32)
    grad_w_out = jnp.dot(mixed.T, grad_attn, preferred_element_type=F32)
    grad_mixed = jnp.einsum("ld,cd->lc", grad_attn, wo, preferred_element_type=F32).astype(BF16)
    inner_sum = jnp.sum(
        (grad_mixed.astype(F32) * mixed.astype(F32)).reshape(n_tok, heads, HDIM), -1
    )
    grad_mixed = grad_mixed.reshape(n_tok, heads, HDIM)
    grad_probs = jnp.einsum("qhe,khe->hqk", grad_mixed, v_all, preferred_element_type=F32)
    grad_scores = (probs.astype(F32) * (grad_probs - inner_sum.T[:, :, None])).astype(BF16)
    grad_v = jnp.einsum("hqk,qhe->khe", probs, grad_mixed, preferred_element_type=F32)
    grad_q = jnp.einsum("hqk,khe->qhe", grad_scores, k_all, preferred_element_type=F32) * att_scale
    grad_k = jnp.einsum("hqk,qhe->khe", grad_scores, q, preferred_element_type=F32)

    def both_cores(g):
        g = g.reshape(2, n_tok, heads, HDIM)
        mine = lax.dynamic_index_in_dim(g, core, 0, keepdims=False)
        send = lax.dynamic_index_in_dim(g, 1 - core, 0, keepdims=False)
        return mine + net.pair(send.astype(BF16), 0).astype(F32)

    grad_k = both_cores(grad_k)
    grad_v = both_cores(grad_v)
    grad_qkv = jnp.stack(
        [
            rotate_back(grad_q, cosine, sine_table),
            rotate_back(grad_k, cosine, sine_table),
            grad_v,
        ],
        1,
    )
    grad_qkv = grad_qkv.astype(BF16).reshape(n_tok, 3, nmp, lw)
    grad_b_qkv = jnp.sum(grad_qkv, 0, dtype=F32)
    grad_w_qkv = jnp.einsum("ltme,ld->mted", grad_qkv, normed_one, preferred_element_type=F32)
    first = jnp.einsum("ltme,mted->ld", grad_qkv, wq, preferred_element_type=F32)
    grad_ln1_gain = jnp.sum(first * unit1, 0)
    grad_ln1_bias = jnp.sum(first, 0)
    grad_x = (grad_residual + norm_back(first, unit1, scale1, ln1_gain)).astype(BF16)
    grad_inputs = net.from_rows([grad_x[:local_len], grad_x[local_len:]]).astype(F32)
    packed = net.reduce_grad(
        jnp.concatenate(
            [grad_w_qkv.reshape(nmp, 3 * lw, width), grad_w_out.reshape(nmp, lw, width)], 1
        )
    )
    grad_w_qkv = jnp.swapaxes(packed[: 3 * lw].reshape(3, lw, width), 1, 2)
    grad_w_out = packed[3 * lw :]

    vec = jnp.concatenate(
        [
            grad_ln1_gain,
            grad_ln1_bias,
            grad_b_out,
            grad_ln2_gain,
            grad_ln2_bias,
            grad_b_down,
            net.by_mp([jnp.swapaxes(grad_b_qkv, 0, 1)[s] for s in (0, 2, 1, 3)]).reshape(-1),
            net.by_mp([grad_b_up[s] for s in (0, 2, 1, 3)]).reshape(-1),
        ]
    )
    vec = lax.psum(vec, ("dp", "mp"))
    reps = [vec[i * width : (i + 1) * width] for i in range(6)]
    rest = vec[6 * width :]
    bq = rest[: 3 * nmp * lw].reshape(nmp, 3, lw)
    bu = rest[3 * nmp * lw :].reshape(nmp, -1)
    grad_b_qkv = lax.dynamic_index_in_dim(bq, z, 0, keepdims=False)
    grad_b_up = lax.dynamic_index_in_dim(bu, z, 0, keepdims=False)
    return (
        layer_out,
        grad_inputs,
        reps[0],
        reps[1],
        grad_w_qkv,
        grad_b_qkv,
        grad_w_out,
        reps[2],
        reps[3],
        reps[4],
        grad_w_up,
        grad_b_up,
        grad_w_down,
        reps[5],
    )


def solution(mesh):
    return jax.shard_map(
        body,
        mesh=mesh,
        in_specs=(
            P("dp", "mp", None),
            P("dp"),
            P(),
            P(),
            P(None, None, "mp"),
            P(None, "mp"),
            P("mp", None),
            P(),
            P(),
            P(),
            P(None, "mp"),
            P("mp"),
            P("mp", None),
            P(),
            P("dp", "mp", None),
        ),
        out_specs=(
            P("dp", "mp", None),
            P("dp", "mp", None),
            P(),
            P(),
            P(None, None, "mp"),
            P(None, "mp"),
            P("mp", None),
            P(),
            P(),
            P(),
            P(None, "mp"),
            P("mp"),
            P("mp", None),
            P(),
        ),
        check_vma=False,
    )
```

```python
import functools
import math

import jax
import jax.numpy as jnp
from jax import lax
from jax.experimental import pallas as pl
from jax.experimental.pallas import tpu as pltpu
from jax.sharding import PartitionSpec as P

HDIM = 64
norm_eps = 1e-05
masked_score = -1000000000.0
F32 = jnp.float32
BF16 = jnp.bfloat16
MESH = pl.DeviceIdType.MESH
NT = (((1,), (1,)), ((), ()))
NN = (((1,), (0,)), ((), ()))
TN = (((0,), (0,)), ((), ()))
ANY = pl.BlockSpec(memory_space=pl.ANY)
VMEM = pl.BlockSpec(memory_space=pltpu.VMEM)


def dot(a, b, form):
    return lax.dot_general(a, b, form, preferred_element_type=F32)


def lanes(i):
    return pl.ds(pl.multiple_of(i * 128, 128), 128)


class Place:
    def __init__(self):
        self.dp = lax.axis_index("dp")
        self.z = lax.axis_index("mp")
        self.b0 = self.dp % 2
        self.b1 = (self.dp // 2) % 2
        self.b2 = (self.dp // 4) % 2
        dp, z = self.dp, self.z
        self.core = (dp + 1 - 2 * self.b0, z)
        self.d1 = (dp + 2 - 4 * self.b1, z)
        self.d2 = (dp + 4 - 8 * self.b2, z)
        self.z1 = (dp, z + 1 - 2 * (z % 2))
        self.z2 = (dp, z + 2 - 4 * (z // 2))
        base = dp - self.b0 + z // 2
        self.row0 = (base, 2 * self.b0 + z % 2)
        self.row1 = (base, 2 * self.b0 + 1 - z % 2)
        self.stays = self.b0 == z // 2
        self.far = []
        step = 8
        while step < lax.axis_size("dp"):
            self.far.append((dp + step - 2 * step * ((dp // step) % 2), z))
            step *= 2

    def greet(self, row_partners, far=False):
        barrier = pltpu.get_barrier_semaphore()
        peers = [self.core, self.d1, self.d2, self.z1, self.z2] + (self.far if far else [])
        if row_partners:
            peers.append(self.row1)
        for peer in peers:
            pl.semaphore_signal(barrier, inc=1, device_id=peer, device_id_type=MESH)
        count = len(peers)
        if row_partners:
            moves = jnp.where(self.stays, 0, 1)
            count = count + moves

            @pl.when(moves == 1)
            def _():
                pl.semaphore_signal(barrier, inc=1, device_id=self.row0, device_id_type=MESH)

        pl.semaphore_wait(barrier, count)


class Sender:
    def __init__(self, send_sems, recv_sems):
        self.send_sems, self.recv_sems = send_sems, recv_sems
        self.used = 0
        self.sent = []

    def remote(self, src, dst, peer, later=True):
        copy = self.copy(self.used, src, dst, peer)
        self.used += 1
        copy.start()
        if later:
            self.sent.append(copy)
        return copy

    def copy(self, i, src, dst, peer):
        return pltpu.make_async_remote_copy(
            src_ref=src,
            dst_ref=dst,
            send_sem=self.send_sems.at[i],
            recv_sem=self.recv_sems.at[i],
            device_id=peer,
            device_id_type=MESH,
        )

    def local(self, src, dst):
        i = self.used
        self.used += 1
        copy = pltpu.make_async_copy(src, dst, self.recv_sems.at[i])
        copy.start()
        return copy

    def finish(self):
        assert self.used <= self.send_sems.shape[0]
        for copy in self.sent:
            copy.wait_send()


class RowMove:
    def __init__(self, here, sender, src0, src1, dst):
        self.here, self.sender = here, sender
        i = sender.used
        sender.used += 1
        self.keep = pltpu.make_async_copy(src0, dst, sender.recv_sems.at[i])
        self.first = sender.copy(i, src0, dst, here.row0)

        @pl.when(here.stays)
        def _():
            self.keep.start()

        @pl.when(jnp.logical_not(here.stays))
        def _():
            self.first.start()

        self.second = sender.remote(src1, dst, here.row1, False)

    def wait(self):
        @pl.when(self.here.stays)
        def _():
            self.keep.wait()

        @pl.when(jnp.logical_not(self.here.stays))
        def _():
            self.first.wait()

        self.second.wait()


class Gather:
    def __init__(self, here, sender, own, ref):
        self.here, self.sender, self.own, self.ref = here, sender, own, ref
        n = ref.shape[1]
        self.half = n // 2
        self.eighth = n // 8
        self.piece = n // 16
        h = here
        start = h.b0 * self.half
        self.rows = [
            start + h.b2 * self.eighth + h.b1 * self.piece,
            start + self.half // 2 + h.b1 * self.eighth + h.b2 * self.piece,
        ]
        self.pairs = [start + h.b2 * self.eighth, start + self.half // 2 + h.b1 * self.eighth]
        self.flying = []

    def ds(self, start, size):
        return pl.ds(pl.multiple_of(start, 16), size)

    def land(self):
        for copy in self.flying:
            copy.wait_recv()
        self.flying = []

    def begin(self):
        for r in self.rows:
            at = self.ds(r, self.piece)
            self.flying.append(
                self.sender.remote(self.own.at[at], self.ref.at[1, at], self.here.z2)
            )

    def step_z1(self):
        for r in self.rows:
            at = self.ds(r, self.piece)
            self.flying.append(
                self.sender.remote(self.own.at[at], self.ref.at[2, at], self.here.z1)
            )
        first, self.flying = self.flying[:2], self.flying[2:]
        for copy in first:
            copy.wait_recv()
        for r in self.rows:
            at = self.ds(r, self.piece)
            self.flying.append(
                self.sender.remote(self.ref.at[1, at], self.ref.at[3, at], self.here.z1)
            )

    def spread(self, at, peer):
        view = self.ref.at[pl.ds(1, 3), at]
        self.flying.append(self.sender.remote(view, view, peer))

    def step_d1(self):
        self.land()
        self.spread(self.ds(self.rows[0], self.piece), self.here.d1)
        self.spread(self.ds(self.rows[1], self.piece), self.here.d2)

    def step_d2(self):
        self.land()
        self.spread(self.ds(self.pairs[0], self.eighth), self.here.d2)
        self.spread(self.ds(self.pairs[1], self.eighth), self.here.d1)

    def step_core(self):
        self.land()
        self.spread(self.ds(self.here.b0 * self.half, self.half), self.here.core)


def normalize(values):
    middle = jnp.mean(values, axis=-1, keepdims=True)
    centred = values - middle
    spread = jnp.mean(centred * centred, axis=-1, keepdims=True)
    scale = lax.rsqrt(spread + norm_eps)
    return centred * scale, scale


def low_half():
    return lax.broadcasted_iota(jnp.int32, (1, 128), 1) % 64 < 32


def rotate_lanes(values, cosine, signed_sine):
    turned = jnp.where(low_half(), pltpu.roll(values, 96, 1), pltpu.roll(values, 32, 1))
    return values * cosine + turned * signed_sine


def first_kernel(
    inputs,
    cotangent,
    lens,
    own_one,
    own_up,
    own_down,
    small,
    vectors,
    x_out,
    n1_out,
    q_out,
    k_out,
    v_out,
    p_out,
    mixed_out,
    res_out,
    n2_out,
    w1_out,
    up_out,
    down_out,
    small_out,
    cot_out,
    len_out,
    cos_out,
    sin_out,
    xbuf,
    n1,
    q,
    k_all,
    v_all,
    probs,
    mixed,
    res,
    n2,
    w1,
    smalls,
    length_ref,
    cots,
    cosine,
    sine,
    send_sems,
    recv_sems,
):
    here = Place()
    net = Sender(send_sems, recv_sems)
    n_tok, width = n1.shape
    half_tok = n_tok // 2
    total = k_all.shape[0]
    lw = (w1.shape[1] * 3 // 4) // 3
    c, z = here.b0, here.z
    with jax.named_scope("greet"):
        here.greet(True)
    one = Gather(here, net, own_one, w1)
    up = Gather(here, net, own_up, up_out)
    down = Gather(here, net, own_down, down_out)
    one.begin()
    own_copy = net.local(own_one, w1.at[0])
    slot = z % 2
    arrive_x = RowMove(
        here, net, inputs.at[z % 2], inputs.at[1 - z % 2], xbuf.at[slot]
    )
    arrive_len = net.remote(lens.at[1 - z % 2], length_ref, here.row1)
    small_own = net.local(small, smalls.at[0])
    small_a = net.remote(small, smalls.at[1], here.z2)

    lane = lax.broadcasted_iota(jnp.int32, (1, 128), 1)
    frequency = jnp.exp((lane % 32).astype(F32) * (-2.0 * math.log(10000.0) / HDIM))

    def tables(i, carry):
        at = pl.ds(pl.multiple_of(i * 64, 64), 64)
        place = c * n_tok + i * 64 + lax.broadcasted_iota(jnp.int32, (64, 1), 0)
        angles = place.astype(F32) * frequency
        cosine[at, :] = jnp.cos(angles)
        sine[at, :] = jnp.where(low_half(), -1.0, 1.0) * jnp.sin(angles)
        return carry

    with jax.named_scope("tables"):
        lax.fori_loop(0, n_tok // 64, tables, 0)

    with jax.named_scope("one_z1"):
        one.step_z1()
    small_own.wait()
    small_a.wait_recv()
    small_b = net.remote(smalls.at[pl.ds(0, 2)], smalls.at[pl.ds(2, 2)], here.z1)
    with jax.named_scope("one_d1"):
        one.step_d1()
    up.begin()
    down.begin()
    with jax.named_scope("one_d2"):
        one.step_d2()
    with jax.named_scope("wait_x"):
        arrive_x.wait()
    x_copy = net.local(xbuf, x_out)

    def norm_one(i, carry):
        for b in range(2):
            at = pl.ds(pl.multiple_of(i * 64, 64), 64)
            unit, _ = normalize(xbuf[b, at, :].astype(F32))
            to = pl.ds(pl.multiple_of(b * half_tok + i * 64, 64), 64)
            n1[to, :] = (unit * vectors[0:1, :] + vectors[1:2, :]).astype(BF16)
        return carry

    with jax.named_scope("norm_one"):
        lax.fori_loop(0, half_tok // 64, norm_one, 0)
    n1_copy = net.local(n1, n1_out)
    with jax.named_scope("one_core"):
        one.step_core()
    with jax.named_scope("ud_z1"):
        up.step_z1()
        down.step_z1()
    small_b.wait_recv()
    with jax.named_scope("one_land"):
        one.land()
        own_copy.wait()
    w1_copy = net.local(w1, w1_out)
    mine = pl.ds(pl.multiple_of(c * n_tok, n_tok), n_tok)

    def bias_of(t):
        rest = lw - 128
        parts = []
        for s in range(4):
            parts.append(smalls[s, 2 * t : 2 * t + 1, :])
            parts.append(smalls[s, 2 * t + 1 : 2 * t + 2, 0:rest])
        return jnp.concatenate(parts, 1)

    def qkv_of(t):
        rows = jnp.concatenate([w1[s, t * lw : (t + 1) * lw, :] for s in range(4)], 0)
        return dot(n1[...], rows, NT) + bias_of(t)

    with jax.named_scope("proj_k"):
        raw = qkv_of(1)
    for i in range(width // 128):
        part = raw[:, i * 128 : (i + 1) * 128]
        k_all[mine, i * 128 : (i + 1) * 128] = rotate_lanes(
            part, cosine[...], sine[...]
        ).astype(BF16)
    move_k = net.remote(k_all.at[mine], k_all.at[mine], here.core)
    with jax.named_scope("proj_v"):
        v_all[mine, :] = qkv_of(2).astype(BF16)
    move_v = net.remote(v_all.at[mine], v_all.at[mine], here.core)
    with jax.named_scope("ud_d1"):
        up.step_d1()
        down.step_d1()
    arrive_cot = RowMove(
        here, net, cotangent.at[z % 2], cotangent.at[1 - z % 2], cots.at[slot]
    )
    raw = qkv_of(0)
    for i in range(width // 128):
        part = raw[:, i * 128 : (i + 1) * 128]
        turned = rotate_lanes(part, cosine[...], sine[...]).astype(BF16)
        q[:, i * 128 : (i + 1) * 128] = turned * jnp.asarray(HDIM**-0.5, BF16)
    q_copy = net.local(q, q_out)
    with jax.named_scope("wait_kv"):
        move_k.wait_recv()
        move_v.wait_recv()
    k_copy = net.local(k_all, k_out)
    v_copy = net.local(v_all, v_out)
    arrive_len.wait_recv()
    len_copy = net.local(length_ref, len_out)
    cos_copy = net.local(cosine, cos_out)
    sin_copy = net.local(sine, sin_out)
    small_copy = net.local(smalls, small_out)

    tile = 256
    first_lanes = lax.broadcasted_iota(jnp.int32, (1, 128), 1) < HDIM
    p_sem = net.used
    net.used += 2

    def p_move(i, s):
        return pltpu.make_async_copy(
            probs.at[s], p_out.at[pl.ds(2 * i, 2)], recv_sems.at[p_sem + s]
        )

    def pair(i, carry):
        s = i % 2

        @pl.when(i >= 2)
        def _():
            p_move(i - 2, s).wait()

        key_place = lax.broadcasted_iota(jnp.int32, (1, total), 1).astype(F32)
        mask = key_place < length_ref[0:1, 0:1]
        kp = k_all[:, lanes(i)]
        vp = v_all[:, lanes(i)]
        for t in range(n_tok // tile):
            at = pl.ds(t * tile, tile)
            sums = 0.0
            for h in range(2):
                chosen = first_lanes if h == 0 else jnp.logical_not(first_lanes)
                kh = jnp.where(chosen, kp, 0)
                vh = jnp.where(chosen, vp, 0)
                scores = jnp.where(mask, dot(q[at, lanes(i)], kh, NT), masked_score)
                top = jnp.max(scores, 1, keepdims=True)
                weights = jnp.exp(scores - top)
                part = (weights * (1.0 / jnp.sum(weights, 1, keepdims=True))).astype(BF16)
                probs[s, h, at, :] = part
                sums = sums + dot(part, vh, NN)
            mixed[at, lanes(i)] = sums.astype(BF16)
        p_move(i, s).start()
        return carry

    pairs = width // 128
    with jax.named_scope("attend_a"):
        lax.fori_loop(0, 2, pair, 0)
    with jax.named_scope("up_d2"):
        up.step_d2()
    with jax.named_scope("attend_b"):
        lax.fori_loop(2, 3, pair, 0)
    with jax.named_scope("down_d2"):
        down.step_d2()
    with jax.named_scope("attend_c"):
        lax.fori_loop(3, 5, pair, 0)
    with jax.named_scope("up_core"):
        up.step_core()
    with jax.named_scope("attend_d"):
        lax.fori_loop(5, pairs, pair, 0)
    mixed_copy = net.local(mixed, mixed_out)
    wo = jnp.concatenate([w1[s, 3 * lw : 4 * lw, :] for s in range(4)], 0)
    with jax.named_scope("project_out"):
        res[...] = dot(mixed[...], wo, NN)

    def norm_two(i, carry):
        for b in range(2):
            at = pl.ds(pl.multiple_of(i * 64, 64), 64)
            to = pl.ds(pl.multiple_of(b * half_tok + i * 64, 64), 64)
            value = xbuf[b, at, :].astype(F32) + (res[to, :] + vectors[2:3, :])
            res[to, :] = value
            unit, _ = normalize(value)
            n2[to, :] = (unit * vectors[3:4, :] + vectors[4:5, :]).astype(BF16)
        return carry

    with jax.named_scope("norm_two"):
        lax.fori_loop(0, half_tok // 64, norm_two, 0)
    with jax.named_scope("down_core"):
        down.step_core()
    copies = [net.local(res, res_out), net.local(n2, n2_out)]
    for i in range(pairs - 2, pairs):
        p_move(i, i % 2).wait()
    copies += [x_copy, n1_copy, w1_copy, q_copy, k_copy, v_copy, len_copy, small_copy, mixed_copy]
    copies += [cos_copy, sin_copy]
    with jax.named_scope("last_waits"):
        for copy in copies:
            copy.wait()
        arrive_cot.wait()
        cot_copy = net.local(cots, cot_out)
        up.land()
        down.land()
        net.finish()
        cot_copy.wait()


def first_part(inputs, cotangent, lengths, own_one, w_up, w_down, small, vectors):
    _, local_len, width = inputs.shape
    n_tok = 2 * local_len
    total = 4 * local_len
    heads = width // HDIM
    n = own_one.shape[0]
    lens = jnp.broadcast_to(lengths.astype(F32)[:, None, None], (2, 8, 128))
    sds = jax.ShapeDtypeStruct
    outs = (
        sds((2, local_len, width), BF16),
        sds((n_tok, width), BF16),
        sds((n_tok, width), BF16),
        sds((total, width), BF16),
        sds((total, width), BF16),
        sds((heads, n_tok, total), BF16),
        sds((n_tok, width), BF16),
        sds((n_tok, width), F32),
        sds((n_tok, width), BF16),
        sds((4, n, width), BF16),
        sds((4,) + w_up.shape, BF16),
        sds((4,) + w_down.shape, BF16),
        sds((4,) + small.shape, F32),
        sds((2, local_len, width), BF16),
        sds((8, 128), F32),
        sds((n_tok, 128), F32),
        sds((n_tok, 128), F32),
    )
    scratch = [
        pltpu.VMEM((2, local_len, width), BF16),
        pltpu.VMEM((n_tok, width), BF16),
        pltpu.VMEM((n_tok, width), BF16),
        pltpu.VMEM((total, width), BF16),
        pltpu.VMEM((total, width), BF16),
        pltpu.VMEM((2, 2, n_tok, total), BF16),
        pltpu.VMEM((n_tok, width), BF16),
        pltpu.VMEM((n_tok, width), F32),
        pltpu.VMEM((n_tok, width), BF16),
        pltpu.VMEM((4, n, width), BF16),
        pltpu.VMEM((4,) + small.shape, F32),
        pltpu.VMEM((8, 128), F32),
        pltpu.VMEM((2, local_len, width), BF16),
        pltpu.VMEM((n_tok, 128), F32),
        pltpu.VMEM((n_tok, 128), F32),
        pltpu.SemaphoreType.DMA((64,)),
        pltpu.SemaphoreType.DMA((64,)),
    ]
    return pl.pallas_call(
        first_kernel,
        out_shape=outs,
        in_specs=[ANY] * 7 + [VMEM],
        out_specs=[ANY] * len(outs),
        scratch_shapes=scratch,
        compiler_params=pltpu.CompilerParams(
            collective_id=1, has_side_effects=True, vmem_limit_bytes=56 * 2**20
        ),
        name="forward_attention",
    )(inputs, cotangent, lens, own_one, w_up, w_down, small, vectors)


class Reduce:
    def __init__(self, here, net, grad, from_core, parts_a, parts_b, parts_z, parts_far, out):
        self.here, self.net, self.grad, self.out = here, net, grad, out
        self.from_core, self.parts_a, self.parts_b = from_core, parts_a, parts_b
        self.parts_z, self.parts_far = parts_z, parts_far
        n = grad.shape[1]
        self.half, self.eighth, self.piece = n // 2, n // 8, n // 16
        h = here
        start = h.b0 * self.half
        middle = start + self.half // 2
        self.keep_half = start
        self.send_half = (1 - h.b0) * self.half
        self.keep_a = [start + h.b2 * self.eighth, middle + h.b1 * self.eighth]
        self.send_a = [start + (1 - h.b2) * self.eighth, middle + (1 - h.b1) * self.eighth]
        self.keep_b = [self.keep_a[0] + h.b1 * self.piece, self.keep_a[1] + h.b2 * self.piece]
        self.send_b = [
            self.keep_a[0] + (1 - h.b1) * self.piece,
            self.keep_a[1] + (1 - h.b2) * self.piece,
        ]
        self.peer_a = [h.d2, h.d1]
        self.peer_b = [h.d1, h.d2]
        self.sems = net.used
        net.used += 4 + 8 + 8
        self.late = []

    def ds(self, start, size):
        return pl.ds(pl.multiple_of(start, 16), size)

    def core_copy(self, s):
        return self.net.copy(
            self.sems + s,
            self.grad.at[s, self.ds(self.send_half, self.half)],
            self.from_core.at[s],
            self.here.core,
        )

    def copies_a(self, s):
        return [
            self.net.copy(
                self.sems + 4 + 4 * i + s,
                self.grad.at[s, self.ds(self.send_a[i], self.eighth)],
                self.parts_a.at[s, i],
                self.peer_a[i],
            )
            for i in range(2)
        ]

    def copies_b(self, s):
        return [
            self.net.copy(
                self.sems + 12 + 4 * i + s,
                self.grad.at[s, self.ds(self.send_b[i], self.piece)],
                self.parts_b.at[s, i],
                self.peer_b[i],
            )
            for i in range(2)
        ]

    def add(self, s, start, source, size):
        def some(i, carry):
            at = self.ds(start + i * self.piece, self.piece)
            more = source[pl.ds(pl.multiple_of(i * self.piece, 16), self.piece), :]
            self.grad[s, at, :] = (
                self.grad[s, at, :].astype(F32) + more.astype(F32)
            ).astype(BF16)
            return carry

        lax.fori_loop(0, size // self.piece, some, 0)

    def core_step(self, s):
        self.core_copy(s).start()

    def step_a(self, s):
        self.core_copy(s).wait_recv()
        self.add(s, self.keep_half, self.from_core.at[s], self.half)
        for copy in self.copies_a(s):
            copy.start()

    def step_b(self, s):
        for i, copy in enumerate(self.copies_a(s)):
            copy.wait_recv()
            self.add(s, self.keep_a[i], self.parts_a.at[s, i], self.eighth)
        for copy in self.copies_b(s):
            copy.start()

    def step_c(self, s):
        for i, copy in enumerate(self.copies_b(s)):
            copy.wait_recv()
            self.add(s, self.keep_b[i], self.parts_b.at[s, i], self.piece)

    def land(self):
        for copy in self.late:
            copy.wait_recv()
        self.late = []

    def step_z1(self):
        for i in range(2):
            for s in range(2):
                self.late.append(
                    self.net.remote(
                        self.grad.at[2 + s, self.ds(self.keep_b[i], self.piece)],
                        self.parts_z.at[s, i],
                        self.here.z1,
                    )
                )

    def step_z2(self):
        self.land()
        for i in range(2):
            for s in range(2):
                self.add(s, self.keep_b[i], self.parts_z.at[s, i], self.piece)
            self.late.append(
                self.net.remote(
                    self.grad.at[1, self.ds(self.keep_b[i], self.piece)],
                    self.parts_z.at[2, i],
                    self.here.z2,
                )
            )

    def total(self):
        self.land()
        for i in range(2):
            self.add(0, self.keep_b[i], self.parts_z.at[2, i], self.piece)
        for b, peer in enumerate(self.here.far):
            for i in range(2):
                at = self.ds(self.keep_b[i], self.piece)
                copy = self.net.remote(
                    self.grad.at[0, at], self.parts_far.at[b, i], peer, False
                )
                copy.wait_send()
                copy.wait_recv()
                self.add(0, self.keep_b[i], self.parts_far.at[b, i], self.piece)

    def back(self, start, size, peer):
        view = self.out.at[self.ds(start, size)]
        self.late.append(self.net.remote(view, view, peer))

    def back_one(self):
        self.total()
        for i in range(2):
            at = self.ds(self.keep_b[i], self.piece)
            self.out[at, :] = self.grad[0, at, :]
            self.back(self.keep_b[i], self.piece, self.peer_b[i])

    def back_two(self):
        self.land()
        for i in range(2):
            self.back(self.keep_a[i], self.eighth, self.peer_a[i])

    def back_core(self):
        self.land()
        self.back(self.keep_half, self.half, self.here.core)

    def finish(self):
        for s in range(4):
            for copy in [self.core_copy(s)] + self.copies_a(s) + self.copies_b(s):
                copy.wait_send()


def second_kernel(
    x_in,
    n1_in,
    q_in,
    k_in,
    v_in,
    p_in,
    mixed_in,
    res_in,
    n2_in,
    w1_in,
    own_up,
    up_in,
    own_down,
    down_in,
    small_in,
    cot_in,
    len_in,
    cos_in,
    sin_in,
    vectors,
    layer_out,
    gin_out,
    one_out,
    up_out,
    down_out,
    vec_out,
    xbuf,
    n1,
    q,
    k_all,
    v_all,
    probs,
    mixed,
    res,
    n2,
    w1,
    w_up,
    w_down,
    smalls,
    gd,
    length_ref,
    cosine,
    sine,
    down_sum,
    gn2,
    act,
    gup,
    gattn,
    gmix,
    lay,
    tbuf,
    gq,
    g_up,
    g_down,
    core_up,
    core_down,
    a_up,
    a_down,
    b_up,
    b_down,
    z_up,
    z_down,
    z_one,
    far_up,
    far_down,
    o_up,
    o_down,
    o_one,
    vec,
    vec_in,
    send_sems,
    recv_sems,
):
    here = Place()
    net = Sender(send_sems, recv_sems)
    n_tok, width = n1.shape
    half_tok = n_tok // 2
    total = k_all.shape[0]
    lw = width // 4
    c, z = here.b0, here.z
    pairs = width // 128
    load = {}
    load["n2"] = net.local(n2_in, n2)
    load["small"] = net.local(small_in, smalls)
    load["len"] = net.local(len_in, length_ref)
    load["gd"] = net.local(cot_in, gd)
    load["up0"] = net.local(own_up, w_up.at[0])
    load["down0"] = net.local(own_down, w_down.at[0])
    slot_sems = net.used
    net.used += 6
    for s in range(1, 4):
        pltpu.make_async_copy(up_in.at[s], w_up.at[s], recv_sems.at[slot_sems + s - 1]).start()
        pltpu.make_async_copy(
            down_in.at[s], w_down.at[s], recv_sems.at[slot_sems + 2 + s]
        ).start()
    load["res"] = net.local(res_in, res)
    load["w1"] = net.local(w1_in, w1)
    load["mixed"] = net.local(mixed_in, mixed)
    load["v"] = net.local(v_in, v_all)
    load["k"] = net.local(k_in, k_all)
    load["q"] = net.local(q_in, q)
    load["cos"] = net.local(cos_in, cosine)
    load["sin"] = net.local(sin_in, sine)
    load["x"] = net.local(x_in, xbuf)
    load["n1"] = net.local(n1_in, n1)
    p_sems = net.used
    net.used += 2

    def p_load(i, s):
        return pltpu.make_async_copy(
            p_in.at[pl.ds(2 * i, 2)], probs.at[s], recv_sems.at[p_sems + s]
        )

    p_load(0, 0).start()
    here.greet(True, True)

    red_up = Reduce(here, net, g_up, core_up, a_up, b_up, z_up, far_up, o_up)
    red_down = Reduce(here, net, g_down, core_down, a_down, b_down, z_down, far_down, o_down)
    both = (red_down, red_up)

    vec[...] = jnp.zeros_like(vec)
    down_sum[...] = jnp.zeros_like(down_sum)
    gn2[...] = jnp.zeros_like(gn2)
    for name in ("len", "gd", "n2", "small"):
        load[name].wait()

    def keep_of(start, size):
        place = c * n_tok + start + lax.broadcasted_iota(jnp.int32, (size, 1), 0)
        return (place.astype(F32) < length_ref[0:1, 0:1]).astype(F32)

    def mask_rows(i, carry):
        at = pl.ds(pl.multiple_of(i * 64, 64), 64)
        kept = gd[at, :].astype(F32) * keep_of(i * 64, 64)
        gd[at, :] = kept.astype(BF16)
        vec[5:6, :] += jnp.sum(kept, 0, keepdims=True)
        return carry

    lax.fori_loop(0, n_tok // 64, mask_rows, 0)
    load["up0"].wait()
    load["down0"].wait()
    tile = 256

    def feed(s, carry):
        @pl.when(s >= 1)
        def _():
            pltpu.make_async_copy(up_in.at[s], w_up.at[s], recv_sems.at[slot_sems + s - 1]).wait()
            pltpu.make_async_copy(
                down_in.at[s], w_down.at[s], recv_sems.at[slot_sems + 2 + s]
            ).wait()

        bias = jnp.concatenate([smalls[s, 8 + i : 9 + i, :] for i in range(pairs)], 1)

        def rows(t, carry):
            at = pl.ds(pl.multiple_of(t * tile, tile), tile)
            up = dot(n2[at, :], w_up[s], NN) + bias
            gact = dot(gd[at, :], w_down[s], NT)
            share = 0.5 * (1.0 + lax.erf(up * 0.7071067811865476))
            slope = share + up * jnp.exp(-0.5 * up * up) * 0.3989422804014327
            active = (up * share).astype(BF16)
            back = (gact * slope).astype(BF16)
            act[at, :] = active
            gup[at, :] = back
            vec[pl.ds(8 + s, 1), :] += jnp.sum(back.astype(F32), 0, keepdims=True)
            down_sum[at, :] += dot(active, w_down[s], NN)
            gn2[at, :] += dot(back, w_up[s], NT)
            return carry

        lax.fori_loop(0, n_tok // tile, rows, 0)
        g_down[s] = dot(act[...], gd[...], TN).astype(BF16)
        red_down.core_step(s)

        @pl.when(s >= 1)
        def _():
            for r in both:
                r.step_a(s - 1)

        g_up[s] = dot(n2[...], gup[...], TN).astype(BF16)
        red_up.core_step(s)

        @pl.when(s >= 2)
        def _():
            for r in both:
                r.step_b(s - 2)

        return carry

    lax.fori_loop(0, 4, feed, 0)
    load["res"].wait()

    def close_feed(i, carry):
        for b in range(2):
            at = pl.ds(pl.multiple_of(i * 64, 64), 64)
            to = pl.ds(pl.multiple_of(b * half_tok + i * 64, 64), 64)
            value = res[to, :]
            kept = (value + (down_sum[to, :] + vectors[5:6, :])) * keep_of(b * half_tok + i * 64, 64)
            lay[b, at, :] = kept.astype(BF16)
            unit, scale = normalize(value)
            g = gn2[to, :]
            h = g * vectors[3:4, :]
            back = scale * (
                h
                - jnp.mean(h, axis=-1, keepdims=True)
                - unit * jnp.mean(h * unit, axis=-1, keepdims=True)
            )
            grad = gd[to, :].astype(F32) + back
            res[to, :] = grad
            low = grad.astype(BF16)
            gattn[to, :] = low
            vec[2:3, :] += jnp.sum(low.astype(F32), 0, keepdims=True)
            vec[3:4, :] += jnp.sum(g * unit, 0, keepdims=True)
            vec[4:5, :] += jnp.sum(g, 0, keepdims=True)
        return carry

    lax.fori_loop(0, half_tok // 64, close_feed, 0)
    slot = z % 2
    move_layer = RowMove(here, net, lay.at[z % 2], lay.at[1 - z % 2], layer_out.at[slot])
    for r in both:
        r.step_a(3)
        r.step_b(2)
    load["w1"].wait()
    load["mixed"].wait()
    wo = jnp.concatenate([w1[s, 3 * lw : 4 * lw, :] for s in range(4)], 0)
    gmix[...] = dot(gattn[...], wo, NT).astype(BF16)
    g_out = dot(mixed[...], gattn[...], TN).astype(BF16)
    for r in both:
        r.step_c(0)
        r.step_c(1)
    g_one = w_up
    swap = w_down
    for s in range(4):
        g_one[s, 3 * lw : 4 * lw, :] = g_out[s * lw : (s + 1) * lw, :]
    for name in ("v", "k", "q", "cos", "sin"):
        load[name].wait()
    gk, gv = down_sum, gn2
    first_lanes = lax.broadcasted_iota(jnp.int32, (1, 128), 1) < HDIM
    mine = pl.ds(pl.multiple_of(c * n_tok, n_tok), n_tok)
    others = pl.ds(pl.multiple_of((1 - c) * n_tok, n_tok), n_tok)

    def pair_back(i, carry):
        s = i % 2

        @pl.when(i + 1 < pairs)
        def _():
            p_load(i + 1, 1 - s).start()

        @pl.when(i == 0)
        def _():
            for r in both:
                r.step_b(3)
                r.step_c(2)

        p_load(i, s).wait()
        kp = k_all[:, lanes(i)]
        vp = v_all[:, lanes(i)]
        gkt = 0.0
        gvt = 0.0
        for t in range(n_tok // tile):
            at = pl.ds(t * tile, tile)
            gm = gmix[at, lanes(i)]
            product = gm.astype(F32) * mixed[at, lanes(i)].astype(F32)
            qp = q[at, lanes(i)]
            gq_sum = 0.0
            for h in range(2):
                chosen = first_lanes if h == 0 else jnp.logical_not(first_lanes)
                inner = jnp.sum(jnp.where(chosen, product, 0.0), 1, keepdims=True)
                gm_h = jnp.where(chosen, gm, 0)
                part = probs[s, h, at, :]
                grad_probs = dot(gm_h, vp, NT)
                scores = (part.astype(F32) * (grad_probs - inner)).astype(BF16)
                gvt = gvt + dot(gm_h, part, TN)
                gkt = gkt + dot(jnp.where(chosen, qp, 0), scores, TN)
                gq_sum = gq_sum + dot(scores, jnp.where(chosen, kp, 0), NN)
            gq[at, lanes(i)] = rotate_lanes(
                gq_sum * HDIM**-0.5, cosine[at, :], -sine[at, :]
            ).astype(BF16)
        tbuf[0] = gkt.T
        tbuf[1] = gvt.T
        gk[:, lanes(i)] = tbuf[0, mine, :]
        gv[:, lanes(i)] = tbuf[1, mine, :]
        swap[0, 0:n_tok, lanes(i)] = tbuf[0, others, :].astype(BF16)
        swap[1, 0:n_tok, lanes(i)] = tbuf[1, others, :].astype(BF16)
        return carry

    def run_pairs(a, b):
        lax.fori_loop(a, b, pair_back, 0)

    run_pairs(0, 1)
    for r in both:
        r.step_c(3)
        r.step_z1()
    run_pairs(1, 2)
    for r in both:
        r.step_z2()
    run_pairs(2, 3)
    for r in both:
        r.back_one()
    run_pairs(3, 5)
    for r in both:
        r.back_two()
    run_pairs(5, 6)
    move_k = net.remote(swap.at[0, pl.ds(0, n_tok)], swap.at[2, pl.ds(0, n_tok)], here.core)
    move_v = net.remote(swap.at[1, pl.ds(0, n_tok)], swap.at[3, pl.ds(0, n_tok)], here.core)
    for r in both:
        r.back_core()

    def weight_of(t):
        return jnp.concatenate([w1[s, t * lw : (t + 1) * lw, :] for s in range(4)], 0)

    load["n1"].wait()
    load["x"].wait()

    def put_grad(t, value):
        grad = dot(value, n1[...], TN).astype(BF16)
        sums = jnp.sum(value.astype(F32), 0, keepdims=True)
        for s in range(4):
            g_one[s, t * lw : (t + 1) * lw, :] = grad[s * lw : (s + 1) * lw, :]
            vec[12 + s : 13 + s, t * lw : (t + 1) * lw] = sums[:, s * lw : (s + 1) * lw]

    put_grad(0, gq[...])
    back_sum = dot(gq[...], weight_of(0), NN)
    move_k.wait_recv()
    for i in range(pairs):
        at = slice(i * 128, (i + 1) * 128)
        whole = gk[:, at] + swap[2, 0:n_tok, at].astype(F32)
        gattn[:, at] = rotate_lanes(whole, cosine[...], -sine[...]).astype(BF16)
    put_grad(1, gattn[...])
    move_v.wait_recv()
    gmix[...] = (gv[...] + swap[3, 0:n_tok, :].astype(F32)).astype(BF16)
    put_grad(2, gmix[...])
    red_one = Reduce(here, net, g_one, core_up, a_up, b_up, z_one, far_up, o_one)
    red_up.finish()
    for s in range(4):
        red_one.core_step(s)
    back_sum = back_sum + dot(gattn[...], weight_of(1), NN)
    gk[...] = back_sum + dot(gmix[...], weight_of(2), NN)
    move_layer.wait()

    def close_first(i, carry):
        for b in range(2):
            at = pl.ds(pl.multiple_of(i * 64, 64), 64)
            to = pl.ds(pl.multiple_of(b * half_tok + i * 64, 64), 64)
            unit, scale = normalize(xbuf[to, :].astype(F32))
            g = gk[to, :]
            h = g * vectors[0:1, :]
            back = scale * (
                h
                - jnp.mean(h, axis=-1, keepdims=True)
                - unit * jnp.mean(h * unit, axis=-1, keepdims=True)
            )
            lay[b, at, :] = (res[to, :] + back).astype(BF16)
            vec[0:1, :] += jnp.sum(g * unit, 0, keepdims=True)
            vec[1:2, :] += jnp.sum(g, 0, keepdims=True)
        return carry

    lax.fori_loop(0, half_tok // 64, close_first, 0)
    move_gin = RowMove(here, net, lay.at[z % 2], lay.at[1 - z % 2], gin_out.at[slot])
    steps = [here.core, here.d1, here.d2] + here.far + [here.z1, here.z2]

    def vec_send(i):
        return net.remote(vec, vec_in.at[i], steps[i], False)

    def vec_add(i, copy):
        copy.wait_send()
        copy.wait_recv()
        if i < len(steps) - 2:
            vec[...] += vec_in[i]
        elif i == len(steps) - 2:
            vec[0:8, :] += vec_in[i, 0:8, :]
            vec[8:10, :] += vec_in[i, 10:12, :]
            vec[12:14, :] += vec_in[i, 14:16, :]
        else:
            vec[0:8, :] += vec_in[i, 0:8, :]
            vec[8:9, :] += vec_in[i, 9:10, :]
            vec[12:13, :] += vec_in[i, 13:14, :]

    flying = vec_send(0)
    for s in range(4):
        red_one.step_a(s)
    vec_add(0, flying)
    flying = vec_send(1)
    red_one.step_b(0)
    red_one.step_b(1)
    vec_add(1, flying)
    flying = vec_send(2)
    red_one.step_b(2)
    red_one.step_b(3)
    for s in range(4):
        red_one.step_c(s)
    red_one.step_z1()
    for i in range(2, len(steps) - 1):
        vec_add(i, flying)
        flying = vec_send(i + 1)
    red_one.step_z2()
    vec_add(len(steps) - 1, flying)
    vec_copy = net.local(vec, vec_out)
    for r in both:
        r.land()
    up_copy = net.local(o_up, up_out)
    down_copy = net.local(o_down, down_out)
    red_one.back_one()
    red_one.back_two()
    red_one.back_core()
    red_one.land()
    one_copy = net.local(o_one, one_out)
    red_down.finish()
    red_one.finish()
    move_gin.wait()
    net.finish()
    for copy in (vec_copy, up_copy, down_copy, one_copy):
        copy.wait()


def second_part(vectors, own_up, own_down, kept):
    (x, n1, q, k_all, v_all, probs, mixed, res, n2, w1, up, down, small, cot, length, cos, sin) = kept
    n_tok, width = n1.shape
    total = k_all.shape[0]
    n = w1.shape[1]
    local_len = n_tok // 2
    sds = jax.ShapeDtypeStruct
    vm = pltpu.VMEM
    far = max(1, lax.axis_size("dp").bit_length() - 4)
    steps = lax.axis_size("dp").bit_length() - 1 + 2
    outs = (
        sds((2, local_len, width), BF16),
        sds((2, local_len, width), BF16),
        sds((n, width), BF16),
        sds((n, width), BF16),
        sds((n, width), BF16),
        sds((16, width), F32),
    )
    tokens = vm((n_tok, width), BF16)
    tokens32 = vm((n_tok, width), F32)
    packet = vm((4, n, width), BF16)
    scratch = [
        tokens,
        tokens,
        tokens,
        vm((total, width), BF16),
        vm((total, width), BF16),
        vm((2, 2, n_tok, total), BF16),
        tokens,
        tokens32,
        tokens,
        packet,
        packet,
        packet,
        vm(small.shape, F32),
        tokens,
        vm((8, 128), F32),
        vm((n_tok, 128), F32),
        vm((n_tok, 128), F32),
        tokens32,
        tokens32,
        tokens,
        tokens,
        tokens,
        tokens,
        vm((2, local_len, width), BF16),
        vm((2, total, 128), F32),
        tokens,
        packet,
        packet,
        vm((4, n // 2, width), BF16),
        vm((4, n // 2, width), BF16),
        vm((4, 2, n // 8, width), BF16),
        vm((4, 2, n // 8, width), BF16),
        vm((4, 2, n // 16, width), BF16),
        vm((4, 2, n // 16, width), BF16),
        vm((3, 2, n // 16, width), BF16),
        vm((3, 2, n // 16, width), BF16),
        vm((3, 2, n // 16, width), BF16),
        vm((far, 2, n // 16, width), BF16),
        vm((far, 2, n // 16, width), BF16),
        vm((n, width), BF16),
        vm((n, width), BF16),
        vm((n, width), BF16),
        vm((16, width), F32),
        vm((steps, 16, width), F32),
        pltpu.SemaphoreType.DMA((160,)),
        pltpu.SemaphoreType.DMA((160,)),
    ]
    args = (
        x, n1, q, k_all, v_all, probs, mixed, res, n2, w1, own_up, up, own_down, down, small, cot,
        length, cos, sin, vectors,
    )
    return pl.pallas_call(
        second_kernel,
        out_shape=outs,
        in_specs=[ANY] * (len(args) - 1) + [VMEM],
        out_specs=[ANY] * len(outs),
        scratch_shapes=scratch,
        compiler_params=pltpu.CompilerParams(
            collective_id=2, has_side_effects=True, vmem_limit_bytes=63 * 2**20
        ),
        name="feed_forward_and_backward",
    )(*args)


def body(
    inputs,
    lengths,
    ln1_gain,
    ln1_bias,
    w_qkv,
    b_qkv,
    w_out,
    b_out,
    ln2_gain,
    ln2_bias,
    w_up,
    b_up,
    w_down,
    b_down,
    cotangent,
):
    local_len, width = inputs.shape[1:]
    lw = w_qkv.shape[2]
    n_tok = 2 * local_len
    w_qkv_t = jnp.swapaxes(w_qkv, 1, 2).reshape(3 * lw, width)
    own_one = jnp.concatenate([w_qkv_t, w_out], 0)
    small = jnp.concatenate(
        [
            jnp.pad(b_qkv, ((0, 0), (0, 256 - lw))).reshape(6, 128),
            jnp.zeros((2, 128), F32),
            b_up.astype(F32).reshape(-1, 128),
            jnp.zeros((2, 128), F32),
        ]
    )
    vectors = jnp.stack([ln1_gain, ln1_bias, b_out, ln2_gain, ln2_bias, b_down, b_down, b_down])
    kept = list(first_part(inputs, cotangent, lengths, own_one, w_up, w_down, small, vectors))
    kept[0] = kept[0].reshape(n_tok, width)
    kept[13] = kept[13].reshape(n_tok, width)
    layer_out, gin, one, up, down, vec = second_part(vectors, w_up, w_down, kept)
    one = one.astype(F32)
    grad_w_qkv = jnp.swapaxes(one[: 3 * lw].reshape(3, lw, width), 1, 2)
    return (
        layer_out,
        gin.astype(F32),
        vec[0],
        vec[1],
        grad_w_qkv,
        vec[12, : 3 * lw].reshape(3, lw),
        one[3 * lw :],
        vec[2],
        vec[3],
        vec[4],
        up.astype(F32),
        vec[8],
        down.astype(F32),
        vec[5],
    )


def solution(mesh):
    return jax.shard_map(
        body,
        mesh=mesh,
        in_specs=(
            P("dp", "mp", None),
            P("dp"),
            P(),
            P(),
            P(None, None, "mp"),
            P(None, "mp"),
            P("mp", None),
            P(),
            P(),
            P(),
            P(None, "mp"),
            P("mp"),
            P("mp", None),
            P(),
            P("dp", "mp", None),
        ),
        out_specs=(
            P("dp", "mp", None),
            P("dp", "mp", None),
            P(),
            P(),
            P(None, None, "mp"),
            P(None, "mp"),
            P("mp", None),
            P(),
            P(),
            P(),
            P(None, "mp"),
            P("mp"),
            P("mp", None),
            P(),
        ),
        check_vma=False,
    )
```

```python
import functools
import math

import jax
import jax.numpy as jnp
from jax import lax
from jax.experimental import pallas as pl
from jax.experimental.pallas import tpu as pltpu
from jax.sharding import PartitionSpec as P

HDIM = 64
norm_eps = 1e-05
masked_score = -1000000000.0
F32 = jnp.float32
BF16 = jnp.bfloat16
MESH = pl.DeviceIdType.MESH
NT = (((1,), (1,)), ((), ()))
NN = (((1,), (0,)), ((), ()))
TN = (((0,), (0,)), ((), ()))
ANY = pl.BlockSpec(memory_space=pl.ANY)
HBM = pl.BlockSpec(memory_space=pltpu.MemorySpace.HBM)
VMEM = pl.BlockSpec(memory_space=pltpu.VMEM)


def dot(a, b, form):
    return lax.dot_general(a, b, form, preferred_element_type=F32)


def lanes(i):
    return pl.ds(pl.multiple_of(i * 128, 128), 128)


class Place:
    def __init__(self):
        self.dp = lax.axis_index("dp")
        self.z = lax.axis_index("mp")
        self.b0 = self.dp % 2
        self.b1 = (self.dp // 2) % 2
        self.b2 = (self.dp // 4) % 2
        dp, z = self.dp, self.z
        self.core = (dp + 1 - 2 * self.b0, z)
        self.d1 = (dp + 2 - 4 * self.b1, z)
        self.d2 = (dp + 4 - 8 * self.b2, z)
        self.z1 = (dp, z + 1 - 2 * (z % 2))
        self.z2 = (dp, z + 2 - 4 * (z // 2))
        base = dp - self.b0 + z // 2
        self.row0 = (base, 2 * self.b0 + z % 2)
        self.row1 = (base, 2 * self.b0 + 1 - z % 2)
        self.stays = self.b0 == z // 2
        self.far = []
        step = 8
        while step < lax.axis_size("dp"):
            self.far.append((dp + step - 2 * step * ((dp // step) % 2), z))
            step *= 2

    def greet(self, row_partners, far=False):
        barrier = pltpu.get_barrier_semaphore()
        peers = [self.core, self.d1, self.d2, self.z1, self.z2] + (self.far if far else [])
        if row_partners:
            peers.append(self.row1)
        for peer in peers:
            pl.semaphore_signal(barrier, inc=1, device_id=peer, device_id_type=MESH)
        count = len(peers)
        if row_partners:
            moves = jnp.where(self.stays, 0, 1)
            count = count + moves

            @pl.when(moves == 1)
            def _():
                pl.semaphore_signal(barrier, inc=1, device_id=self.row0, device_id_type=MESH)

        pl.semaphore_wait(barrier, count)


class Sender:
    def __init__(self, send_sems, recv_sems):
        self.send_sems, self.recv_sems = send_sems, recv_sems
        self.used = 0
        self.sent = []

    def remote(self, src, dst, peer, later=True):
        copy = self.copy(self.used, src, dst, peer)
        self.used += 1
        copy.start()
        if later:
            self.sent.append(copy)
        return copy

    def copy(self, i, src, dst, peer):
        return pltpu.make_async_remote_copy(
            src_ref=src,
            dst_ref=dst,
            send_sem=self.send_sems.at[i],
            recv_sem=self.recv_sems.at[i],
            device_id=peer,
            device_id_type=MESH,
        )

    def local(self, src, dst):
        i = self.used
        self.used += 1
        copy = pltpu.make_async_copy(src, dst, self.recv_sems.at[i])
        copy.start()
        return copy

    def finish(self):
        assert self.used <= self.send_sems.shape[0]
        for copy in self.sent:
            copy.wait_send()


class RowMove:
    def __init__(self, here, sender, src0, src1, dst):
        self.here, self.sender = here, sender
        i = sender.used
        sender.used += 1
        self.keep = pltpu.make_async_copy(src0, dst, sender.recv_sems.at[i])
        self.first = sender.copy(i, src0, dst, here.row0)

        @pl.when(here.stays)
        def _():
            self.keep.start()

        @pl.when(jnp.logical_not(here.stays))
        def _():
            self.first.start()

        self.second = sender.remote(src1, dst, here.row1, False)

    def wait(self):
        @pl.when(self.here.stays)
        def _():
            self.keep.wait()

        @pl.when(jnp.logical_not(self.here.stays))
        def _():
            self.first.wait()

        self.second.wait()


class Gather:
    def __init__(self, here, sender, own, ref, begin, n):
        self.here, self.sender, self.own, self.ref = here, sender, own, ref
        w = ref.shape[2]
        self.cols = [pl.ds(0, w // 2), pl.ds(w // 2, w // 2)]
        self.half, self.quarter, self.piece = n // 2, n // 4, n // 8
        h = here
        self.start = begin + h.b0 * self.half
        self.pairs = [self.start + h.b2 * self.quarter, self.start + h.b1 * self.quarter]
        self.rows = [self.pairs[0] + h.b1 * self.piece, self.pairs[1] + h.b2 * self.piece]
        self.flying = []
        self.sent = []

    def ds(self, start, size):
        return pl.ds(pl.multiple_of(start, 16), size)

    def land(self):
        for copy in self.flying:
            copy.wait_recv()
        self.flying = []

    def send(self, source, target, peer):
        copy = self.sender.remote(source, target, peer, False)
        self.flying.append(copy)
        self.sent.append(copy)

    def finish(self):
        self.land()
        for copy in self.sent:
            copy.wait_send()

    def over_z(self, source, target, peer):
        for r, cols in zip(self.rows, self.cols):
            at = self.ds(r, self.piece)
            self.send(source.at[at, cols], self.ref.at[target, at, cols], peer)

    def step_z2(self):
        self.over_z(self.own, 1, self.here.z2)

    def step_z1(self):
        first, self.flying = self.flying, []
        self.over_z(self.own, 2, self.here.z1)
        for copy in first:
            copy.wait_recv()
        self.over_z(self.ref.at[1], 3, self.here.z1)

    def spread(self, at, cols, peer):
        view = self.ref.at[pl.ds(1, 3), at, cols]
        self.send(view, view, peer)

    def step_d1(self):
        self.land()
        self.spread(self.ds(self.rows[0], self.piece), self.cols[0], self.here.d1)
        self.spread(self.ds(self.rows[1], self.piece), self.cols[1], self.here.d2)

    def step_d2(self):
        self.land()
        self.spread(self.ds(self.pairs[0], self.quarter), self.cols[0], self.here.d2)
        self.spread(self.ds(self.pairs[1], self.quarter), self.cols[1], self.here.d1)

    def step_core(self):
        self.land()
        view = self.ref.at[pl.ds(1, 3), self.ds(self.start, self.half)]
        self.send(view, view, self.here.core)


def normalize(values):
    middle = jnp.mean(values, axis=-1, keepdims=True)
    centred = values - middle
    spread = jnp.mean(centred * centred, axis=-1, keepdims=True)
    scale = lax.rsqrt(spread + norm_eps)
    return centred * scale, scale


def low_half():
    return lax.broadcasted_iota(jnp.int32, (1, 128), 1) % 64 < 32


def rotate_lanes(values, cosine, signed_sine):
    turned = jnp.where(low_half(), pltpu.roll(values, 96, 1), pltpu.roll(values, 32, 1))
    return values * cosine + turned * signed_sine


class Reduce:
    unit = 48

    def __init__(self, here, net, grad, begin, n, groups, from_core, parts_a, parts_b, parts_z, parts_far, out):
        self.here, self.net, self.grad, self.out, self.groups = here, net, grad, out, groups
        self.from_core, self.parts_a, self.parts_b = from_core, parts_a, parts_b
        self.parts_z, self.parts_far = parts_z, parts_far
        w = grad.shape[2]
        self.cols = [pl.ds(0, w // 2), pl.ds(w // 2, w // 2)]
        self.half, self.quarter, self.piece = n // 2, n // 4, n // 8
        h = here
        start = begin + h.b0 * self.half
        self.keep_half = start
        self.send_half = begin + (1 - h.b0) * self.half
        self.keep_a = [start + h.b2 * self.quarter, start + h.b1 * self.quarter]
        self.send_a = [start + (1 - h.b2) * self.quarter, start + (1 - h.b1) * self.quarter]
        self.keep_b = [self.keep_a[0] + h.b1 * self.piece, self.keep_a[1] + h.b2 * self.piece]
        self.send_b = [
            self.keep_a[0] + (1 - h.b1) * self.piece,
            self.keep_a[1] + (1 - h.b2) * self.piece,
        ]
        self.peer_a = [h.d2, h.d1]
        self.peer_b = [h.d1, h.d2]
        self.sems = net.used
        net.used += 5 * len(groups)
        self.late = []
        self.kept = []

    def ds(self, start, size):
        return pl.ds(pl.multiple_of(start, 16), size)

    def core_copies(self, g):
        first, count = self.groups[g]
        at = pl.ds(first, count)
        return [
            self.net.copy(
                self.sems + 5 * g,
                self.grad.at[at, self.ds(self.send_half, self.half)],
                self.from_core(first, count),
                self.here.core,
            )
        ]

    def copies_a(self, g):
        first, count = self.groups[g]
        at = pl.ds(first, count)
        return [
            self.net.copy(
                self.sems + 5 * g + 1 + i,
                self.grad.at[at, self.ds(self.send_a[i], self.quarter), self.cols[i]],
                self.parts_a.at[at, i],
                self.peer_a[i],
            )
            for i in range(2)
        ]

    def copies_b(self, g):
        first, count = self.groups[g]
        at = pl.ds(first, count)
        return [
            self.net.copy(
                self.sems + 5 * g + 3 + i,
                self.grad.at[at, self.ds(self.send_b[i], self.piece), self.cols[i]],
                self.parts_b.at[at, i],
                self.peer_b[i],
            )
            for i in range(2)
        ]

    def add(self, s, start, cols, source, size):
        def some(i, carry):
            at = self.ds(start + i * self.unit, self.unit)
            more = source[pl.ds(pl.multiple_of(i * self.unit, 16), self.unit), :]
            self.grad[s, at, cols] = (
                self.grad[s, at, cols].astype(F32) + more.astype(F32)
            ).astype(BF16)
            return carry

        lax.fori_loop(0, size // self.unit, some, 0)

    def slots(self, g):
        first, count = self.groups[g]
        return range(first, first + count)

    def step_core(self, g):
        for copy in self.core_copies(g):
            copy.start()

    def step_a(self, g):
        for copy in self.core_copies(g):
            copy.wait_recv()
        for s in self.slots(g):
            self.add(s, self.keep_half, slice(None), self.from_core(s, 1).at[0], self.half)
        for copy in self.copies_a(g):
            copy.start()

    def step_b(self, g):
        for i, copy in enumerate(self.copies_a(g)):
            copy.wait_recv()
            for s in self.slots(g):
                self.add(s, self.keep_a[i], self.cols[i], self.parts_a.at[s, i], self.quarter)
        for copy in self.copies_b(g):
            copy.start()

    def step_c(self, g):
        for i, copy in enumerate(self.copies_b(g)):
            copy.wait_recv()
            for s in self.slots(g):
                self.add(s, self.keep_b[i], self.cols[i], self.parts_b.at[s, i], self.piece)

    def land(self):
        for copy in self.late:
            copy.wait_recv()
        self.late = []

    def mine(self, i):
        return self.ds(self.keep_b[i], self.piece), self.cols[i]

    def step_z1(self):
        for i in range(2):
            at, cols = self.mine(i)
            self.late.append(
                self.net.remote(
                    self.grad.at[pl.ds(2, 2), at, cols],
                    self.parts_z.at[pl.ds(0, 2), i],
                    self.here.z1,
                )
            )

    def step_z2(self):
        self.land()
        for i in range(2):
            at, cols = self.mine(i)
            for s in (1, 0):
                self.add(s, self.keep_b[i], cols, self.parts_z.at[s, i], self.piece)
            self.late.append(
                self.net.remote(self.grad.at[1, at, cols], self.parts_z.at[2, i], self.here.z2)
            )

    def total(self):
        self.land()
        for i in range(2):
            self.add(0, self.keep_b[i], self.cols[i], self.parts_z.at[2, i], self.piece)
        for b, peer in enumerate(self.here.far):
            for i in range(2):
                at, cols = self.mine(i)
                copy = self.net.remote(
                    self.grad.at[0, at, cols], self.parts_far.at[b, i], peer, False
                )
                copy.wait_send()
                copy.wait_recv()
                self.add(0, self.keep_b[i], cols, self.parts_far.at[b, i], self.piece)

    def back(self, view, peer):
        self.late.append(self.net.remote(view, view, peer))

    def back_one(self):
        self.total()
        for i in range(2):
            at, cols = self.mine(i)
            source, target = self.grad.at[0, at, cols], self.out.at[at, cols]
            self.kept.append(self.net.local(source, target))
            self.late.append(self.net.remote(source, target, self.peer_b[i]))

    def back_two(self):
        self.land()
        for copy in self.kept:
            copy.wait()
        for i in range(2):
            at = self.ds(self.keep_a[i], self.quarter)
            self.back(self.out.at[at, self.cols[i]], self.peer_a[i])

    def back_core(self):
        self.land()
        self.back(self.out.at[self.ds(self.keep_half, self.half)], self.here.core)

    def finish(self):
        for g in range(len(self.groups)):
            for copy in self.core_copies(g) + self.copies_a(g) + self.copies_b(g):
                copy.wait_send()


ORDER = (
    "w_z2 tab o_z2 w_z1",
    "u_z2 o_z1 w_d1 d_z2",
    "o_d1 u_z1 x_start o_d2",
    "w_d2 u_d1 o_core u_d2",
    "d_z1 small w_core ln",
    "kproj vproj c_start kv",
    "qproj d_d1 p0 u_core",
    "p1 d_d2 p2 p3",
    "p4 p5 out d_core",
    "f0r f0d f0u f1r",
    "f1d U0_A f1u f2r",
    "D1_A U1_A f2d f2u",
    "f3r f3d U2_A f3u",
    "close gm U0_B U3_A",
    "q0 U2_B D2_A q1",
    "q2 U3_B D3_A U2_c",
    "sw0 q3 D2_B q4",
    "U1_B q5 sw1 U3_c",
    "U_z1 U0_c D1_B D3_B",
    "wo D0_A U1_c D2_c",
    "sw gv W1_C gq",
    "W0_C D3_c D_z1 gk",
    "U_z2 W1_A W0_A bs",
    "cf O0_C D0_B D1_c",
    "O0_A W1_B v0 D0_c",
    "D_z2 O1_C W0_B O1_A",
    "v1 v2 W0_c W_z1",
    "O0_B U_b1 O1_B O0_c",
    "W1_c D_b1 O_z1 O1_c",
    "U_b2 W_z2 D_b2 O_z2",
    "v3 W_b1 O_b1 D_b3",
    "U_b3 v4 W_b2 O_b2",
    "W_b3 O_b3",
)


def steps_in_order():
    for line in ORDER:
        yield from line.split()


def layer_kernel(
    inputs,
    cotangent,
    w_qkv,
    w_out,
    own_up,
    own_down,
    lengths,
    b_qkv,
    b_up,
    ln1_gain,
    ln1_bias,
    b_out,
    ln2_gain,
    ln2_bias,
    b_down,
    layer_out,
    gin_out,
    one_out,
    up_out,
    down_out,
    vec_out,
    p_hbm,
    xbuf,
    n1,
    q,
    k_all,
    v_all,
    probs,
    mixed,
    res,
    n2,
    w1,
    w_up,
    w_down,
    smalls,
    lens,
    length_ref,
    gd,
    cosine,
    sine,
    down_sum,
    gn2,
    act,
    gup,
    gattn,
    lay,
    tbuf,
    shares,
    g_up,
    g_down,
    core_up,
    core_down,
    a_up,
    a_down,
    a_one,
    a_two,
    from_b_up,
    from_b_down,
    from_b_one,
    from_b_two,
    z_up,
    z_down,
    z_one,
    z_two,
    far_up,
    far_down,
    far_one,
    far_two,
    vec,
    vec_in,
    send_sems,
    recv_sems,
):
    here = Place()
    net = Sender(send_sems, recv_sems)
    n_tok, width = n1.shape
    half_tok = n_tok // 2
    total = k_all.shape[0]
    pairs = width // 128
    lw = width // 4
    c, z = here.b0, here.z
    slot = z % 2
    tile = 256
    held = {}
    step = {}
    ends = []

    def row(vector):
        return vector[...].reshape(1, width)

    def blocks(body, count, size):
        def one(i, carry):
            body(pl.multiple_of(i * size, size))
            return carry

        lax.fori_loop(0, count, one, 0)

    own = [net.local(w_qkv, w1.at[0, pl.ds(0, 3 * lw)])]
    own.append(net.local(w_out, w1.at[0, pl.ds(3 * lw, lw)]))
    own_ff = [net.local(own_up, w_up.at[0]), net.local(own_down, w_down.at[0])]
    smalls[...] = jnp.zeros_like(smalls)
    for t in range(3):
        smalls[0, 2 * t : 2 * t + 1, :] = b_qkv[t : t + 1, 0:128]
        smalls[0, 2 * t + 1 : 2 * t + 2, 0 : lw - 128] = b_qkv[t : t + 1, 128:lw]
    up_bias = b_up[...].reshape(1, width).astype(F32)
    for i in range(pairs):
        smalls[0, 8 + i : 9 + i, :] = up_bias[:, i * 128 : (i + 1) * 128]
    for j in range(2):
        lens[j] = jnp.full(lens.shape[1:], lengths[j].astype(F32))
    vec[...] = jnp.zeros_like(vec)
    shares[...] = jnp.zeros_like(shares)
    for copy in own:
        copy.wait()
    here.greet(True, True)
    arrive_len = net.remote(lens.at[1 - z % 2], length_ref, here.row1)
    small_a = net.remote(smalls.at[0], smalls.at[1], here.z2)

    gathers = {
        "o": Gather(here, net, w1.at[0], w1, 0, 2 * lw),
        "w": Gather(here, net, w1.at[0], w1, 2 * lw, 2 * lw),
        "u": Gather(here, net, own_up, w_up, 0, 4 * lw),
        "d": Gather(here, net, own_down, w_down, 0, 4 * lw),
    }
    for name, g in gathers.items():
        step[name + "_z2"] = g.step_z2
        step[name + "_z1"] = g.step_z1
        step[name + "_d1"] = g.step_d1
        step[name + "_d2"] = g.step_d2
        step[name + "_core"] = g.step_core

    def small():
        small_a.wait_recv()
        held["small"] = net.remote(smalls.at[pl.ds(0, 2)], smalls.at[pl.ds(2, 2)], here.z1)

    step["small"] = small

    def arrive(name, source, target):
        def begin():
            to = target.at[pl.ds(pl.multiple_of(slot * half_tok, half_tok), half_tok)]
            held[name] = RowMove(here, net, source.at[z % 2], source.at[1 - z % 2], to)

        step[name + "_start"] = begin

    arrive("x", inputs, xbuf)
    arrive("c", cotangent, gd)

    def tables():
        lane = lax.broadcasted_iota(jnp.int32, (1, 128), 1)
        frequency = jnp.exp((lane % 32).astype(F32) * (-2.0 * math.log(10000.0) / HDIM))

        def some(r):
            place = c * n_tok + r + lax.broadcasted_iota(jnp.int32, (64, 1), 0)
            angles = place.astype(F32) * frequency
            cosine[pl.ds(r, 64), :] = jnp.cos(angles)
            sine[pl.ds(r, 64), :] = jnp.where(low_half(), -1.0, 1.0) * jnp.sin(angles)

        blocks(some, n_tok // 64, 64)

    step["tab"] = tables

    def norm_one():
        held["x"].wait()

        def some(r):
            unit, _ = normalize(xbuf[pl.ds(r, 64), :].astype(F32))
            n1[pl.ds(r, 64), :] = (unit * row(ln1_gain) + row(ln1_bias)).astype(BF16)

        blocks(some, n_tok // 64, 64)

    step["ln"] = norm_one
    mine = pl.ds(pl.multiple_of(c * n_tok, n_tok), n_tok)
    others = pl.ds(pl.multiple_of((1 - c) * n_tok, n_tok), n_tok)

    def weight_of(t):
        return jnp.concatenate([w1[s, t * lw : (t + 1) * lw, :] for s in range(4)], 0)

    def qkv_of(t):
        parts = []
        for s in range(4):
            parts.append(smalls[s, 2 * t : 2 * t + 1, :])
            parts.append(smalls[s, 2 * t + 1 : 2 * t + 2, 0 : lw - 128])
        return dot(n1[...], weight_of(t), NT) + jnp.concatenate(parts, 1)

    def k_part():
        held["small"].wait_recv()
        gathers["o"].land()
        raw = qkv_of(1)
        for i in range(pairs):
            at = slice(i * 128, (i + 1) * 128)
            k_all[mine, at] = rotate_lanes(raw[:, at], cosine[...], sine[...]).astype(BF16)
        held["k"] = net.remote(k_all.at[mine], k_all.at[mine], here.core)

    def v_part():
        gathers["w"].land()
        v_all[mine, :] = qkv_of(2).astype(BF16)
        held["v"] = net.remote(v_all.at[mine], v_all.at[mine], here.core)

    def q_part():
        raw = qkv_of(0)
        for i in range(pairs):
            at = slice(i * 128, (i + 1) * 128)
            turned = rotate_lanes(raw[:, at], cosine[...], sine[...]).astype(BF16)
            q[:, at] = turned * jnp.asarray(HDIM**-0.5, BF16)

    step["kproj"], step["vproj"], step["qproj"] = k_part, v_part, q_part
    head_lane = lax.broadcasted_iota(jnp.int32, (1, 128), 1)
    first_lanes = head_lane < HDIM
    p_sems = net.used
    net.used += 4

    def p_store(i, s):
        return pltpu.make_async_copy(
            probs.at[s], p_hbm.at[pl.ds(2 * i, 2)], recv_sems.at[p_sems + s]
        )

    def p_load(i, s):
        return pltpu.make_async_copy(
            p_hbm.at[pl.ds(2 * i, 2)], probs.at[s], recv_sems.at[p_sems + 2 + s]
        )

    def pair(i, carry):
        s = i % 2

        @pl.when(i >= 2)
        def _():
            p_store(i - 2, s).wait()

        key_place = lax.broadcasted_iota(jnp.int32, (1, total), 1).astype(F32)
        mask = key_place < length_ref[0:1, 0:1]
        kp = k_all[:, lanes(i)]
        vp = v_all[:, lanes(i)]
        heads = [jnp.where(first_lanes, kp, 0), jnp.where(first_lanes, 0, kp)]
        values = [jnp.where(first_lanes, vp, 0), jnp.where(first_lanes, 0, vp)]
        order = [(t, h) for t in range(n_tok // tile) for h in range(2)]

        def score(t, h):
            return dot(q[pl.ds(t * tile, tile), lanes(i)], heads[h], NT)

        ahead = score(*order[0])
        for j, (t, h) in enumerate(order):
            at = pl.ds(t * tile, tile)
            scores = jnp.where(mask, ahead, masked_score)
            if j + 1 < len(order):
                ahead = score(*order[j + 1])
            weights = jnp.exp(scores - jnp.max(scores, 1, keepdims=True))
            part = 1.0 / jnp.sum(weights, 1, keepdims=True)
            low = weights.astype(BF16)
            probs[s, h, at, :] = low
            shares[at, :] = jnp.where(head_lane == 2 * i + h, part, shares[at, :])
            product = dot(low, values[h], NN) * part
            sums = product if h == 0 else sums + product
            if h == 1:
                mixed[at, lanes(i)] = sums.astype(BF16)
        p_store(i, s).start()
        return carry

    def attend():
        held["k"].wait_recv()
        held["v"].wait_recv()
        arrive_len.wait_recv()

    step["kv"] = attend
    for i in range(pairs):
        step["p" + str(i)] = functools.partial(lax.fori_loop, i, i + 1, pair, 0)

    def norm_two():
        wo = jnp.concatenate([w1[s, 3 * lw : 4 * lw, :] for s in range(4)], 0)
        res[...] = dot(mixed[...], wo, NN)

        def some(r):
            at = pl.ds(r, 64)
            value = xbuf[at, :].astype(F32) + (res[at, :] + row(b_out))
            res[at, :] = value
            unit, _ = normalize(value)
            n2[at, :] = (unit * row(ln2_gain) + row(ln2_bias)).astype(BF16)

        blocks(some, n_tok // 64, 64)
        for i in range(pairs - 2, pairs):
            p_store(i, i % 2).wait()
        p_load(0, 0).start()

    step["out"] = norm_two

    g_one = w_up
    swap = w_down
    n = 4 * lw
    each = [(i, 1) for i in range(4)]
    twos = [(2, 2), (0, 2)]

    def at_slots(ref):
        return lambda first, count: ref.at[pl.ds(first, count)]

    def at_probs(begin):
        def some(first, count):
            rows = pl.ds(begin, lw)
            if count == 2:
                return probs.at[first // 2, :, rows, pl.ds(0, width)]
            return probs.at[first // 2, pl.ds(first % 2, 1), rows, pl.ds(0, width)]

        return some

    red_up = Reduce(here, net, g_up, 0, n, each, at_slots(core_up), a_up, from_b_up, z_up, far_up, up_out)
    red_down = Reduce(here, net, g_down, 0, n, each, at_slots(core_down), a_down, from_b_down, z_down, far_down, down_out)
    red_one = Reduce(here, net, g_one, 0, n // 2, twos, at_probs(0), a_one, from_b_one, z_one, far_one, one_out)
    red_two = Reduce(here, net, g_one, n // 2, n // 2, twos, at_probs(lw), a_two, from_b_two, z_two, far_two, one_out)
    for name, r in (("U", red_up), ("D", red_down), ("O", red_one), ("W", red_two)):
        for g in range(len(r.groups)):
            step[name + str(g) + "_A"] = functools.partial(r.step_a, g)
            step[name + str(g) + "_B"] = functools.partial(r.step_b, g)
            step[name + str(g) + "_c"] = functools.partial(r.step_c, g)
            if r in (red_one, red_two):
                step[name + str(g) + "_C"] = functools.partial(r.step_core, g)
        step[name + "_z1"], step[name + "_z2"] = r.step_z1, r.step_z2
        step[name + "_b1"], step[name + "_b2"] = r.back_one, r.back_two
        step[name + "_b3"] = r.back_core

    def keep_of(start, size):
        place = c * n_tok + start + lax.broadcasted_iota(jnp.int32, (size, 1), 0)
        return (place.astype(F32) < length_ref[0:1, 0:1]).astype(F32)

    def before_feed():
        held["c"].wait()
        down_sum[...] = jnp.zeros_like(down_sum)
        gn2[...] = jnp.zeros_like(gn2)

        def some(r):
            kept = gd[pl.ds(r, 64), :].astype(F32) * keep_of(r, 64)
            gd[pl.ds(r, 64), :] = kept.astype(BF16)
            vec[5:6, :] += jnp.sum(kept, 0, keepdims=True)

        blocks(some, n_tok // 64, 64)
        for copy in own_ff:
            copy.wait()

    def feed_rows(s):
        if s == 0:
            before_feed()
        if s == 1:
            gathers["u"].finish()
            gathers["d"].finish()
        bias = jnp.concatenate([smalls[s, 8 + i : 9 + i, :] for i in range(pairs)], 1)

        def some(r):
            at = pl.ds(r, tile)
            up = dot(n2[at, :], w_up[s], NN) + bias
            gact = dot(gd[at, :], w_down[s], NT)
            share = 0.5 * (1.0 + lax.erf(up * 0.7071067811865476))
            slope = share + up * jnp.exp(-0.5 * up * up) * 0.3989422804014327
            active = (up * share).astype(BF16)
            back = (gact * slope).astype(BF16)
            act[at, :] = active
            gup[at, :] = back
            vec[8 + s : 9 + s, :] += jnp.sum(back.astype(F32), 0, keepdims=True)
            down_sum[at, :] += dot(active, w_down[s], NN)
            gn2[at, :] += dot(back, w_up[s], NT)

        for t in range(n_tok // tile):
            some(t * tile)

    def feed_down(s):
        g_down[s] = dot(act[...], gd[...], TN).astype(BF16)
        red_down.step_core(s)

    def feed_up(s):
        g_up[s] = dot(n2[...], gup[...], TN).astype(BF16)
        red_up.step_core(s)

    for s in range(4):
        step["f" + str(s) + "r"] = functools.partial(feed_rows, s)
        step["f" + str(s) + "d"] = functools.partial(feed_down, s)
        step["f" + str(s) + "u"] = functools.partial(feed_up, s)

    def norm_back(unit, scale, g, gain):
        h = g * gain
        return scale * (
            h
            - jnp.mean(h, axis=-1, keepdims=True)
            - unit * jnp.mean(h * unit, axis=-1, keepdims=True)
        )

    def close_feed():
        def some(r):
            for b in range(2):
                to = pl.ds(pl.multiple_of(b * half_tok + r, 64), 64)
                value = res[to, :]
                kept = (value + (down_sum[to, :] + row(b_down))) * keep_of(b * half_tok + r, 64)
                lay[b, pl.ds(r, 64), :] = kept.astype(BF16)
                unit, scale = normalize(value)
                g = gn2[to, :]
                grad = gd[to, :].astype(F32) + norm_back(unit, scale, g, row(ln2_gain))
                res[to, :] = grad
                low = grad.astype(BF16)
                gattn[to, :] = low
                vec[2:3, :] += jnp.sum(low.astype(F32), 0, keepdims=True)
                vec[3:4, :] += jnp.sum(g * unit, 0, keepdims=True)
                vec[4:5, :] += jnp.sum(g, 0, keepdims=True)

        blocks(some, half_tok // 64, 64)
        held["lay"] = RowMove(here, net, lay.at[z % 2], lay.at[1 - z % 2], layer_out.at[slot])

    step["close"] = close_feed

    gq, gmix = act, gup
    def mix_back():
        wo = jnp.concatenate([w1[s, 3 * lw : 4 * lw, :] for s in range(4)], 0)
        gmix[...] = dot(gattn[...], wo, NT).astype(BF16)

    def out_back():
        grad = dot(mixed[...], gattn[...], TN).astype(BF16)
        for s in range(4):
            g_one[s, 3 * lw : 4 * lw, :] = grad[s * lw : (s + 1) * lw, :]

    step["gm"], step["wo"] = mix_back, out_back
    gk, gv = down_sum, gn2

    def pair_back(i, carry):
        s = i % 2

        @pl.when(i + 1 < pairs)
        def _():
            p_load(i + 1, 1 - s).start()

        p_load(i, s).wait()
        kp = k_all[:, lanes(i)]
        vp = v_all[:, lanes(i)]
        gkt = 0.0
        gvt = 0.0
        for t in range(n_tok // tile):
            at = pl.ds(t * tile, tile)
            part = [
                jnp.sum(jnp.where(head_lane == 2 * i + h, shares[at, :], 0.0), 1, keepdims=True)
                for h in range(2)
            ]
            scaled = gmix[at, lanes(i)].astype(F32) * jnp.where(first_lanes, part[0], part[1])
            gm = scaled.astype(BF16)
            product = scaled * mixed[at, lanes(i)].astype(F32)
            qp = q[at, lanes(i)]
            gq_sum = 0.0
            for h in range(2):
                chosen = first_lanes if h == 0 else jnp.logical_not(first_lanes)
                inner = jnp.sum(jnp.where(chosen, product, 0.0), 1, keepdims=True)
                gm_h = jnp.where(chosen, gm, 0)
                weights = probs[s, h, at, :]
                grad_probs = dot(gm_h, vp, NT)
                scores = (weights.astype(F32) * (grad_probs - inner)).astype(BF16)
                gvt = gvt + dot(gm_h, weights, TN)
                gkt = gkt + dot(jnp.where(chosen, qp, 0), scores, TN)
                gq_sum = gq_sum + dot(scores, jnp.where(chosen, kp, 0), NN)
            gq[at, lanes(i)] = rotate_lanes(
                gq_sum * HDIM**-0.5, cosine[at, :], -sine[at, :]
            ).astype(BF16)
        tbuf[0] = gkt.T
        tbuf[1] = gvt.T
        gk[:, lanes(i)] = tbuf[0, mine, :]
        gv[:, lanes(i)] = tbuf[1, mine, :]
        swap[0, 0:n_tok, lanes(i)] = tbuf[0, others, :].astype(BF16)
        swap[1, 0:n_tok, lanes(i)] = tbuf[1, others, :].astype(BF16)
        return carry

    for i in range(pairs):
        step["q" + str(i)] = functools.partial(lax.fori_loop, i, i + 1, pair_back, 0)

    def swap_part(i):
        at = pl.ds(i * (width // 2), width // 2)
        here_at = pl.ds(0, n_tok)
        held["sw" + str(i)] = [
            net.remote(swap.at[j, here_at, at], swap.at[2 + j, here_at, at], here.core)
            for j in range(2)
        ]

    step["sw0"], step["sw1"] = functools.partial(swap_part, 0), functools.partial(swap_part, 1)

    def put_grad(t, value):
        grad = dot(value, n1[...], TN).astype(BF16)
        sums = jnp.sum(value.astype(F32), 0, keepdims=True)
        for s in range(4):
            g_one[s, t * lw : (t + 1) * lw, :] = grad[s * lw : (s + 1) * lw, :]
            vec[12 + s : 13 + s, t * lw : (t + 1) * lw] = sums[:, s * lw : (s + 1) * lw]

    def q_back():
        put_grad(0, gq[...])

    def swaps():
        for copy in held["sw0"] + held["sw1"]:
            copy.wait_recv()

    step["sw"] = swaps

    def k_back():
        for i in range(pairs):
            at = slice(i * 128, (i + 1) * 128)
            whole = gk[:, at] + swap[2, 0:n_tok, at].astype(F32)
            gattn[:, at] = rotate_lanes(whole, cosine[...], -sine[...]).astype(BF16)
        put_grad(1, gattn[...])

    def v_back():
        gmix[...] = (gv[...] + swap[3, 0:n_tok, :].astype(F32)).astype(BF16)
        put_grad(2, gmix[...])

    def sum_back():
        sums = dot(gq[...], weight_of(0), NN) + dot(gattn[...], weight_of(1), NN)
        gk[...] = sums + dot(gmix[...], weight_of(2), NN)

    step["gq"], step["gk"], step["gv"] = q_back, k_back, v_back
    step["bs"] = sum_back

    def close_first():
        held["lay"].wait()

        def some(r):
            for b in range(2):
                to = pl.ds(pl.multiple_of(b * half_tok + r, 64), 64)
                unit, scale = normalize(xbuf[to, :].astype(F32))
                g = gk[to, :]
                grad = res[to, :] + norm_back(unit, scale, g, row(ln1_gain))
                lay[b, pl.ds(r, 64), :] = grad.astype(BF16)
                vec[0:1, :] += jnp.sum(g * unit, 0, keepdims=True)
                vec[1:2, :] += jnp.sum(g, 0, keepdims=True)

        blocks(some, half_tok // 64, 64)
        held["gin"] = RowMove(here, net, lay.at[z % 2], lay.at[1 - z % 2], gin_out.at[slot])

    step["cf"] = close_first

    peers = [here.core, here.d1, here.d2] + here.far + [here.z1, here.z2]

    def vec_send(i):
        held["vec"] = net.remote(vec, vec_in.at[i], peers[i], False)

    def vec_add(i):
        held["vec"].wait_send()
        held["vec"].wait_recv()
        if i < len(peers) - 2:
            vec[...] += vec_in[i]
            return
        a = 2 if i == len(peers) - 2 else 1
        vec[0:8, :] += vec_in[i, 0:8, :]
        vec[8 : 8 + a, :] += vec_in[i, 8 + a : 8 + 2 * a, :]
        vec[12 : 12 + a, :] += vec_in[i, 12 + a : 12 + 2 * a, :]

    def vec_step(i):
        if i > 0:
            vec_add(i - 1)
        vec_send(i)
        if i == 2:
            for j in range(len(here.far)):
                vec_add(i + j)
                vec_send(i + j + 1)

    def vec_last(i):
        n = len(peers) - 2 + i
        vec_add(n - 1)
        vec_send(n)

    for i in range(3):
        step["v" + str(i)] = functools.partial(vec_step, i)
    step["v3"], step["v4"] = functools.partial(vec_last, 0), functools.partial(vec_last, 1)

    done = list(steps_in_order())
    assert sorted(done) == sorted(step)
    for name in done:
        step[name]()
    vec_add(len(peers) - 1)
    ends.append(net.local(vec, vec_out))
    red_down.land()
    red_up.land()
    held["gin"].wait()
    red_one.land()
    red_two.land()
    for r in (gathers["o"], gathers["w"], red_up, red_down, red_one, red_two):
        r.finish()
    net.finish()
    for copy in ends:
        copy.wait()


def whole_layer(inputs, cotangent, lengths, w_qkv, w_out, w_up, w_down, b_qkv, b_up, vectors):
    _, local_len, width = inputs.shape
    n_tok = 2 * local_len
    total = 4 * local_len
    heads = width // HDIM
    lw = w_out.shape[0]
    n = 4 * lw
    sds = jax.ShapeDtypeStruct
    vm = pltpu.VMEM
    far = max(1, lax.axis_size("dp").bit_length() - 4)
    hops = lax.axis_size("dp").bit_length() - 1 + 2
    outs = (
        sds((2, local_len, width), BF16),
        sds((2, local_len, width), BF16),
        sds((n, width), BF16),
        sds((n, width), BF16),
        sds((n, width), BF16),
        sds((16, width), F32),
        sds((heads, n_tok, total), BF16),
    )
    tokens = vm((n_tok, width), BF16)
    tokens32 = vm((n_tok, width), F32)
    packet = vm((4, n, width), BF16)
    piece = n // 8
    scratch = [
        tokens,
        tokens,
        tokens,
        vm((total, width), BF16),
        vm((total, width), BF16),
        vm((2, 2, n_tok, total), BF16),
        tokens,
        tokens32,
        tokens,
        packet,
        packet,
        packet,
        vm((4, 16, 128), F32),
        vm((2, 8, 128), F32),
        vm((8, 128), F32),
        tokens,
        vm((n_tok, 128), F32),
        vm((n_tok, 128), F32),
        tokens32,
        tokens32,
        tokens,
        tokens,
        tokens,
        vm((2, local_len, width), BF16),
        vm((2, total, 128), F32),
        vm((n_tok, 128), F32),
        packet,
        packet,
        vm((4, n // 2, width), BF16),
        vm((4, n // 2, width), BF16),
        *[vm((4, 2, k * piece, width // 2), BF16) for k in (2, 2, 1, 1)],
        *[vm((4, 2, k * piece // 2, width // 2), BF16) for k in (2, 2, 1, 1)],
        *[vm((3, 2, k * piece // 2, width // 2), BF16) for k in (2, 2, 1, 1)],
        *[vm((far, 2, k * piece // 2, width // 2), BF16) for k in (2, 2, 1, 1)],
        vm((16, width), F32),
        vm((hops, 16, width), F32),
        pltpu.SemaphoreType.DMA((208,)),
        pltpu.SemaphoreType.DMA((208,)),
    ]
    w_qkv_t = jnp.swapaxes(w_qkv, 1, 2).reshape(3 * lw, width)
    args = (inputs, cotangent, w_qkv_t, w_out, w_up, w_down, lengths, b_qkv, b_up) + vectors
    return pl.pallas_call(
        layer_kernel,
        out_shape=outs,
        in_specs=[ANY] * 6 + [pl.BlockSpec(memory_space=pltpu.SMEM)] + [VMEM] * 8,
        out_specs=[ANY] * len(outs),
        scratch_shapes=scratch,
        compiler_params=pltpu.CompilerParams(
            collective_id=1, has_side_effects=True, vmem_limit_bytes=63 * 2**20
        ),
        name="encoder_layer",
    )(*args)[:-1]


def finish_kernel(layer_in, gin_in, one_in, up_in, down_in, vec, layer, gin, qkv, wo, up, down, reps, b_qkv, b_up,
                  layer_buf, gin_buf, one_buf, up_buf, down_buf, gin32, one32, up32, down32, sems):
    lw = wo.shape[0]
    width = wo.shape[1]
    loads = [(gin_in, gin_buf), (one_in, one_buf), (up_in, up_buf), (down_in, down_buf), (layer_in, layer_buf)]
    loads = [pltpu.make_async_copy(a, b, sems.at[i]) for i, (a, b) in enumerate(loads)]
    for copy in loads:
        copy.start()
    for i, ref in enumerate(reps):
        ref[...] = vec[i : i + 1, :].reshape(width)
    b_up[...] = vec[8:9, :].reshape(width)
    for t in range(3):
        b_qkv[t : t + 1, :] = vec[12:13, t * lw : (t + 1) * lw]
    stores = []

    def store(a, b):
        copy = pltpu.make_async_copy(a, b, sems.at[len(loads) + len(stores)])
        copy.start()
        stores.append(copy)

    def widen(source, target, start, size):
        def some(i, carry):
            at = pl.ds(pl.multiple_of(start + i * 64, 64), 64)
            target[at, :] = source[at, :].astype(F32)
            return carry

        lax.fori_loop(0, size // 64, some, 0)

    loads[0].wait()
    for i in range(2):
        n = gin_buf.shape[0] // 2
        widen(gin_buf, gin32, i * n, n)
        store(gin32.at[pl.ds(i * n, n)], gin.at[pl.ds(i * n, n)])
    loads[4].wait()
    store(layer_buf, layer)
    loads[1].wait()
    widen(one_buf, one32, 0, 3 * lw)
    store(one32.at[pl.ds(0, 3 * lw)], qkv)
    widen(one_buf, one32, 3 * lw, lw)
    store(one32.at[pl.ds(3 * lw, lw)], wo)
    loads[2].wait()
    widen(up_buf, up32, 0, 4 * lw)
    store(up32, up)
    loads[3].wait()
    for i in range(2):
        widen(down_buf, down32, i * 2 * lw, 2 * lw)
        at = pl.ds(i * 2 * lw, 2 * lw)
        store(down32.at[at], down.at[at])
    for copy in stores:
        copy.wait()


def finish_layer(layer_out, gin, one, up, down, vec):
    n, width = one.shape
    lw = n // 4
    rows = gin.shape[0] * gin.shape[1]
    sds = jax.ShapeDtypeStruct
    vm = pltpu.VMEM

    def kernel(*refs):
        finish_kernel(*refs[:12], refs[12:18], *refs[18:])

    outs = [sds((rows, width), BF16), sds((rows, width), F32), sds((3 * lw, width), F32)]
    outs += [sds((lw, width), F32), sds((n, width), F32), sds((n, width), F32)]
    outs += [sds((width,), F32)] * 6 + [sds((3, lw), F32), sds((width,), F32)]
    tokens = vm((rows, width), BF16)
    square = vm((n, width), BF16)
    square32 = vm((n, width), F32)
    got = pl.pallas_call(
        kernel,
        out_shape=tuple(outs),
        in_specs=[HBM] * 5 + [VMEM],
        out_specs=[HBM] * 6 + [VMEM] * 8,
        scratch_shapes=[tokens, tokens, square, square, square, vm((rows, width), F32)]
        + [square32, square32, square32, pltpu.SemaphoreType.DMA((16,))],
        compiler_params=pltpu.CompilerParams(vmem_limit_bytes=63 * 2**20),
        name="outputs",
    )(layer_out.reshape(rows, width), gin.reshape(rows, width), one, up, down, vec)
    return got


def body(
    inputs,
    lengths,
    ln1_gain,
    ln1_bias,
    w_qkv,
    b_qkv,
    w_out,
    b_out,
    ln2_gain,
    ln2_bias,
    w_up,
    b_up,
    w_down,
    b_down,
    cotangent,
):
    width = inputs.shape[2]
    lw = w_qkv.shape[2]
    vectors = (ln1_gain, ln1_bias, b_out, ln2_gain, ln2_bias, b_down)
    layer_out, gin, one, up, down, vec = whole_layer(
        inputs, cotangent, lengths, w_qkv, w_out, w_up, w_down, b_qkv, b_up, vectors
    )
    layer, gin, qkv, wo, up, down, *rest = finish_layer(layer_out, gin, one, up, down, vec)
    return (
        layer.reshape(inputs.shape),
        gin.reshape(inputs.shape),
        rest[0],
        rest[1],
        jnp.swapaxes(qkv.reshape(3, lw, width), 1, 2),
        rest[6],
        wo,
        rest[2],
        rest[3],
        rest[4],
        up,
        rest[7],
        down,
        rest[5],
    )


def solution(mesh):
    return jax.shard_map(
        body,
        mesh=mesh,
        in_specs=(
            P("dp", "mp", None),
            P("dp"),
            P(),
            P(),
            P(None, None, "mp"),
            P(None, "mp"),
            P("mp", None),
            P(),
            P(),
            P(),
            P(None, "mp"),
            P("mp"),
            P("mp", None),
            P(),
            P("dp", "mp", None),
        ),
        out_specs=(
            P("dp", "mp", None),
            P("dp", "mp", None),
            P(),
            P(),
            P(None, None, "mp"),
            P(None, "mp"),
            P("mp", None),
            P(),
            P(),
            P(),
            P(None, "mp"),
            P("mp"),
            P("mp", None),
            P(),
        ),
        check_vma=False,
    )
```
